32 devices in a mesh: grp: 2 (over y), gy: 4 (over z), gz: 2 (over x), wa: 2 (over core).
Axes of the slice: x: 2, y: 2, z: 4, core: 2. Of those that a mesh axis runs over, the one named last changes fastest.
Arguments:
- start: float32 [2, 96, 96, 256], P('grp', 'gy', 'gz', 'wa'), may hold values from 0 to 1
- rates: float32 [8, 2, 96, 96, 256], P(None, 'grp', 'gy', 'gz', 'wa'), may hold values from 0.05 to 1
- labels: int32 [2, 96, 96, 256], P('grp', 'gy', 'gz', 'wa'), may hold values from 0 to 2, as said below
- cotangent: float32 [2, 96, 96, 256], P('grp', 'gy', 'gz', 'wa'), may hold values from -24 to 24
Outputs:
- committor: float32 [2, 96, 96, 256], P('grp', 'gy', 'gz', 'wa')
- grad_start: float32 [2, 96, 96, 256], P('grp', 'gy', 'gz', 'wa')
- grad_rates: float32 [8, 2, 96, 96, 256], P(None, 'grp', 'gy', 'gz', 'wa')
The draws below stay inside these ranges and needn't reach their ends.
Inputs may be any that keep to these rules, and one draw needn't show every extreme that they name: `labels`: 0 marks an interior cell, 1 a reactant milestone cell, 2 a product milestone cell.
All inputs are finite; a program needn't handle non-finite values.
Results may differ from the reference program's by a relative error of at most 0.00002.
Values sent between devices are 32-bit elements; how exact they have to be, the bound alone decides.
No kernel may reach another device: no remote copies, remote signals or barrier semaphores. Data moves between devices by JAX's collectives and lax.ppermute only.
A program may use at most 192 MiB of HBM per device.

```python
import math
import jax
import jax.numpy as jnp

NB = 96
NC = 96
ND = 256
NA = 2


def draw_labels(key, part):
    key = jax.random.fold_in(key, 1)
    picks = jax.random.randint(key, (NA, NB, NC, ND), 0, 16)
    return jnp.where(picks == 0, 1, jnp.where(picks == 1, 2, 0)).astype(jnp.int32)


def steps_of(key, extent, shards, smallest, high):
    gain, own = 1.0, jax.random.fold_in(key, 6)
    for position, parts in shards:
        draws = jnp.exp(jax.random.uniform(jax.random.fold_in(own, position), (parts,), jnp.float32, smallest / len(shards), high / len(shards)))
        gain = gain * jnp.repeat(draws, extent[position] // parts).reshape([-1 if axis == position else 1 for axis in range(len(extent))])
    return gain


def centred(key, dims, scale, bound, split=(), held_as=jnp.bfloat16):
    entries = jax.random.normal(key, dims, jnp.float32) * scale
    if len(split) > 0:
        entries = steps_of(key, dims, split, -0.22, 0.18) * entries
    return jnp.clip(entries, min=-bound, max=bound).astype(held_as)


def setup_inputs(seed: int = 0) -> dict:
    key_of = jax.random.split(jax.random.key(seed), 5)
    return {
        "start": jnp.clip(1.0 * jax.random.uniform(key_of[0], (NA, NB, NC, ND), jnp.float32) ** steps_of(key_of[0], (NA, NB, NC, ND), ((0, 2), (1, 4), (2, 2), (3, 2)), -0.2, 0.2), 0.0, 1.0),
        "rates": jnp.clip(jnp.exp(math.log(1.0) - 2.9957323 * jax.random.uniform(key_of[1], (8, NA, NB, NC, ND), jnp.float32) ** steps_of(key_of[1], (8, NA, NB, NC, ND), ((1, 2), (2, 4), (3, 2), (4, 2)), -0.2, 0.2)), 0.05, 1.0),
        "labels": draw_labels(jax.random.fold_in(key_of[4], 71), 0),
        "cotangent": centred(key_of[3], (NA, NB, NC, ND), 4.0, 24.0, ((0, 2), (1, 4), (2, 2), (3, 2)), jnp.float32),
    }


def sweep(field, weight, interior, product):
    average = jnp.zeros_like(field)
    for d in range(4):
        average = average + weight[2 * d] * jnp.roll(field, -1, d)
        average = average + weight[2 * d + 1] * jnp.roll(field, 1, d)
    return interior * ((1.0 - 0.8) * field + 0.8 * average) + product, average


def adjoint(grad, coeff, interior):
    result = (1.0 - 0.8) * interior * grad
    for d in range(4):
        result = result + jnp.roll(coeff[2 * d] * grad, 1, d)
        result = result + jnp.roll(coeff[2 * d + 1] * grad, -1, d)
    return result


def reference(start, rates, labels, cotangent):
    interior = (labels == 0).astype(jnp.float32)
    product = (labels == 2).astype(jnp.float32)
    total = jnp.sum(rates, axis=0)
    weight = rates / total
    first, avg_zero = sweep(start, weight, interior, product)
    committor, avg_one = sweep(first, weight, interior, product)
    coeff = 0.8 * interior * weight
    back = adjoint(cotangent, coeff, interior)
    grad_start = adjoint(back, coeff, interior)
    factor = 0.8 * interior / total
    pieces = []
    for d in range(4):
        for shift_by in (-1, 1):
            term = cotangent * (jnp.roll(first, shift_by, d) - avg_one)
            term = term + back * (jnp.roll(start, shift_by, d) - avg_zero)
            pieces.append(term * factor)
    return committor, grad_start, jnp.stack(pieces)
```

```python
import functools

import jax
import jax.numpy as jnp
from jax import lax
from jax.experimental import pallas as pl
from jax.experimental.pallas import tpu as pltpu
from jax.sharding import PartitionSpec as P

DAMP = 0.8
KEEP = 1.0 - 0.8


def ring(axis, distance):
    size = lax.axis_size(axis)
    return [(i, (i + distance) % size) for i in range(size)]


def both_ways(up, down, axis):
    if lax.axis_size(axis) == 2 and up is down:
        other = lax.ppermute(up, axis, ring(axis, 1))
        return other, other
    return lax.ppermute(up, axis, ring(axis, 1)), lax.ppermute(down, axis, ring(axis, -1))


def call(body, name, operands, shapes, flops):
    unique, places = [], []
    for x in operands:
        for i, y in enumerate(unique):
            if x is y:
                places.append(i)
                break
        else:
            places.append(len(unique))
            unique.append(x)

    def kernel(*refs):
        ins = [refs[i] for i in places]
        body(*ins, *refs[len(unique):])

    moved = sum(4 * x.size for x in unique) + sum(4 * functools.reduce(lambda a, b: a * b, s) for s in shapes)
    return pl.pallas_call(
        kernel,
        out_shape=[jax.ShapeDtypeStruct(s, jnp.float32) for s in shapes],
        in_specs=[pl.BlockSpec(memory_space=pltpu.VMEM)] * len(unique),
        out_specs=[pl.BlockSpec(memory_space=pltpu.VMEM)] * len(shapes),
        compiler_params=pltpu.CompilerParams(vmem_limit_bytes=40 * 1024 * 1024),
        cost_estimate=pl.CostEstimate(flops=flops, bytes_accessed=moved, transcendentals=0),
        name=name,
    )(*unique)


def iotas(c, d):
    return lax.broadcasted_iota(jnp.int32, (c, d), 0), lax.broadcasted_iota(jnp.int32, (c, d), 1)


def next_c(x, halo, row):
    c = x.shape[0]
    return jnp.where(row == c - 1, halo, pltpu.roll(x, c - 1, 0))


def prev_c(x, halo, row):
    return jnp.where(row == 0, halo, pltpu.roll(x, 1, 0))


def next_d(x, other, lane):
    d = x.shape[1]
    return pltpu.roll(jnp.where(lane == 0, other, x), d - 1, 1)


def prev_d(x, other, lane):
    d = x.shape[1]
    return pltpu.roll(jnp.where(lane == d - 1, other, x), 1, 1)


def prev_b(ref, halo, b):
    return jnp.where(b == 0, halo, ref[0, jnp.maximum(b - 1, 0)])


def next_b(ref, halo, b, count):
    return jnp.where(b == count - 1, halo, ref[0, jnp.minimum(b + 1, count - 1)])


def neighbours(ref, before_b, after_b, gz_before, gz_after, wa_before, wa_after, b, row, lane):
    count = ref.shape[1]
    x = ref[0, b]
    return [
        next_b(ref, after_b[0], b, count),
        prev_b(ref, before_b[0], b),
        next_c(x, gz_after[1, pl.ds(b, 1), :], row),
        prev_c(x, gz_before[0, pl.ds(b, 1), :], row),
        next_d(x, wa_after[0, b], lane),
        prev_d(x, wa_before[0, b], lane),
    ]


def prepare_body(pair, rates, labels, cot, start, f_ref, g_ref, w_ref, up_ref, down_ref, gz_ref, *u_refs):
    count, c, d = g_ref.shape[1:]
    row, lane = iotas(c, d)

    def step(b, _):
        r = [rates[j, 0, b] for j in range(8)]
        total = ((r[0] + r[1]) + (r[2] + r[3])) + ((r[4] + r[5]) + (r[6] + r[7]))
        f = jnp.where(labels[0, b] == 0, DAMP / total, 0.0)
        g = f * cot[0, b]
        f_ref[0, b] = f
        g_ref[0, b] = g
        if pair:
            u_refs[0][0, b] = (r[0] + r[1]) * g
        else:
            u_refs[0][0, b] = r[0] * g
            u_refs[1][0, b] = r[1] * g
        w_ref[0, b] = jnp.where(lane == 0, r[7] * g, r[6] * g)
        gz_ref[0, pl.ds(b, 1), :] = start[0, b, c - 1 :, :]
        gz_ref[1, pl.ds(b, 1), :] = start[0, b, :1, :]
        gz_ref[2, pl.ds(b, 1), :] = (r[4] * g)[c - 1 :]
        gz_ref[3, pl.ds(b, 1), :] = (r[5] * g)[:1]
        return 0

    lax.fori_loop(0, count, step, 0)
    up_ref[0] = start[0, count - 1]
    up_ref[1] = rates[2, 0, count - 1] * g_ref[0, count - 1]
    down_ref[0] = start[0, 0]
    down_ref[1] = rates[3, 0, 0] * g_ref[0, 0]


def forward_body(pair, rates, f_ref, labels, q, q_before, q_after, up, down, gz_before, gz_after, wa_before, wa_after, first, s_ref):
    count, c, d = q.shape[1:]
    row, lane = iotas(c, d)

    def step(b, _):
        f = f_ref[0, b]
        near = neighbours(q, up, down, gz_before, gz_after, wa_before, wa_after, b, row, lane)
        total = sum(rates[2 + k, 0, b] * near[k] for k in range(6))
        if pair:
            total = total + (rates[0, 0, b] + rates[1, 0, b]) * q_after[0, b]
        else:
            total = total + rates[0, 0, b] * q_after[0, b] + rates[1, 0, b] * q_before[0, b]
        s = f * total
        label = labels[0, b]
        s_ref[0, b] = s
        first[0, b] = jnp.where(label == 0, KEEP * q[0, b] + s, jnp.where(label == 2, 1.0, 0.0))
        return 0

    lax.fori_loop(0, count, step, 0)


def spread(rates, f_ref, x, g, up, down, gz_before, gz_after, wa_before, wa_after, at, b, row, lane):
    count, c, d = g.shape[1:]
    f, own = f_ref[0, b], g[0, b]
    below, above = jnp.maximum(b - 1, 0), jnp.minimum(b + 1, count - 1)
    out = jnp.where(f > 0.0, KEEP * x, 0.0)
    out = out + jnp.where(b == 0, up[at], rates[2, 0, below] * g[0, below])
    out = out + jnp.where(b == count - 1, down[at], rates[3, 0, above] * g[0, above])
    out = out + prev_c(rates[4, 0, b] * own, gz_before[2 * at, pl.ds(b, 1), :], row)
    out = out + next_c(rates[5, 0, b] * own, gz_after[2 * at + 1, pl.ds(b, 1), :], row)
    out = out + prev_d(rates[6, 0, b] * own, wa_before[0, b], lane)
    out = out + next_d(rates[7, 0, b] * own, wa_after[0, b], lane)
    return out


def back_body(pair, rates, f_ref, cot, g, u_before, u_after, up, down, gz_before, gz_after, wa_before, wa_after, first,
              back, h_ref, w_ref, up_ref, down_ref, gz_ref, *v_refs):
    count, c, d = g.shape[1:]
    row, lane = iotas(c, d)

    def step(b, _):
        out = spread(rates, f_ref, cot[0, b], g, up, down, gz_before, gz_after, wa_before, wa_after, 1, b, row, lane)
        if pair:
            out = out + u_before[0, b]
        else:
            out = out + u_before[0, b] + u_after[0, b]
        h = f_ref[0, b] * out
        back[0, b] = out
        h_ref[0, b] = h
        if pair:
            v_refs[0][0, b] = (rates[0, 0, b] + rates[1, 0, b]) * h
        else:
            v_refs[0][0, b] = rates[0, 0, b] * h
            v_refs[1][0, b] = rates[1, 0, b] * h
        w_ref[0, b] = jnp.where(lane == 0, rates[7, 0, b] * h, rates[6, 0, b] * h)
        gz_ref[0, pl.ds(b, 1), :] = first[0, b, c - 1 :, :]
        gz_ref[1, pl.ds(b, 1), :] = first[0, b, :1, :]
        gz_ref[2, pl.ds(b, 1), :] = (rates[4, 0, b] * h)[c - 1 :]
        gz_ref[3, pl.ds(b, 1), :] = (rates[5, 0, b] * h)[:1]
        return 0

    lax.fori_loop(0, count, step, 0)
    up_ref[0] = first[0, count - 1]
    up_ref[1] = rates[2, 0, count - 1] * h_ref[0, count - 1]
    down_ref[0] = first[0, 0]
    down_ref[1] = rates[3, 0, 0] * h_ref[0, 0]


def partial_body(rates, f_ref, back, h, up, down, gz_before, gz_after, wa_before, wa_after, out):
    count, c, d = h.shape[1:]
    row, lane = iotas(c, d)

    def step(b, _):
        out[0, b] = spread(rates, f_ref, back[0, b], h, up, down, gz_before, gz_after, wa_before, wa_after, 1, b, row, lane)
        return 0

    lax.fori_loop(0, count, step, 0)


def last_body(rates, f_ref, labels, g, h, s_ref, start, start_before, start_after, up0, down0, gz_before0, gz_after0, wa_before0,
              wa_after0, first, first_before, first_after, up1, down1, gz_before1, gz_after1, wa_before1, wa_after1, committor, out):
    count, c, d = first.shape[1:]
    row, lane = iotas(c, d)

    def step(b, _):
        f = f_ref[0, b]
        near1 = [first_after[0, b], first_before[0, b]]
        near1 += neighbours(first, up1, down1, gz_before1, gz_after1, wa_before1, wa_after1, b, row, lane)
        s1 = f * sum(rates[k, 0, b] * near1[k] for k in range(8))
        label = labels[0, b]
        committor[0, b] = jnp.where(label == 0, KEEP * first[0, b] + s1, jnp.where(label == 2, 1.0, 0.0))
        near0 = [start_after[0, b], start_before[0, b]]
        near0 += neighbours(start, up0, down0, gz_before0, gz_after0, wa_before0, wa_after0, b, row, lane)
        avg1, avg0 = s1 * (1.0 / DAMP), s_ref[0, b] * (1.0 / DAMP)
        gb, hb = g[0, b], h[0, b]
        for k in range(8):
            out[k, 0, b] = gb * (near1[k] - avg1) + hb * (near0[k] - avg0)
        return 0

    lax.fori_loop(0, count, step, 0)


def on_device(start, rates, labels, cotangent):
    _, b, c, d = start.shape
    block = (1, b, c, d)
    cells = b * c * d
    pair = lax.axis_size("grp") == 2
    blocks = [block] * (1 if pair else 2)
    faces = [(2, c, d), (2, c, d), (4, b, d)]

    start_before, start_after = both_ways(start, start, "grp")
    f, g, w0, up, down, gz, *u = call(
        functools.partial(prepare_body, pair), "prepare", [rates, labels, cotangent, start], [block] * 3 + faces + blocks, 20 * cells
    )
    u_before, u_after = both_ways(u[0], u[-1], "grp")
    up0, down0 = both_ways(up, down, "gy")
    gz_before0, gz_after0 = both_ways(gz, gz, "gz")
    wa0 = both_ways(start, start, "wa")
    waw0 = both_ways(w0, w0, "wa")

    first, s0 = call(
        functools.partial(forward_body, pair),
        "forward",
        [rates, f, labels, start, start_before, start_after, up0, down0, gz_before0, gz_after0, *wa0],
        [block] * 2,
        30 * cells,
    )
    first_before, first_after = both_ways(first, first, "grp")
    wa1 = both_ways(first, first, "wa")

    back, h, w1, up, down, gz, *v = call(
        functools.partial(back_body, pair),
        "backward",
        [rates, f, cotangent, g, u_before, u_after, up0, down0, gz_before0, gz_after0, *waw0, first],
        [block] * 3 + faces + blocks,
        30 * cells,
    )
    v_before, v_after = both_ways(v[0], v[-1], "grp")
    up1, down1 = both_ways(up, down, "gy")
    gz_before1, gz_after1 = both_ways(gz, gz, "gz")
    waw1 = both_ways(w1, w1, "wa")

    (grad,) = call(partial_body, "partial", [rates, f, back, h, up1, down1, gz_before1, gz_after1, *waw1], [block], 30 * cells)
    committor, grad_rates = call(
        last_body,
        "last",
        [rates, f, labels, g, h, s0, start, start_before, start_after, up0, down0, gz_before0, gz_after0, *wa0,
         first, first_before, first_after, up1, down1, gz_before1, gz_after1, *wa1],
        [block, (8, 1, b, c, d)],
        90 * cells,
    )
    grad_start = grad + v_before if pair else grad + v_before + v_after
    return committor, grad_start, grad_rates


def solution(mesh):
    placed = (
        P("grp", "gy", "gz", "wa"),
        P(None, "grp", "gy", "gz", "wa"),
        P("grp", "gy", "gz", "wa"),
        P("grp", "gy", "gz", "wa"),
    )
    return jax.shard_map(
        on_device,
        mesh=mesh,
        in_specs=placed,
        out_specs=(
            P("grp", "gy", "gz", "wa"),
            P("grp", "gy", "gz", "wa"),
            P(None, "grp", "gy", "gz", "wa"),
        ),
        check_vma=False,
    )
```

```python
import functools

import jax
import jax.numpy as jnp
from jax import lax
from jax.experimental import pallas as pl
from jax.experimental.pallas import tpu as pltpu
from jax.sharding import PartitionSpec as P

DAMP = 0.8
KEEP = 1.0 - 0.8


def ring(axis, distance):
    size = lax.axis_size(axis)
    return [(i, (i + distance) % size) for i in range(size)]


def both_ways(up, down, axis):
    if lax.axis_size(axis) == 2 and up is down:
        other = lax.ppermute(up, axis, ring(axis, 1))
        return other, other
    return lax.ppermute(up, axis, ring(axis, 1)), lax.ppermute(down, axis, ring(axis, -1))


def call(body, name, operands, shapes, flops):
    unique, places = [], []
    for x in operands:
        for i, y in enumerate(unique):
            if x is y:
                places.append(i)
                break
        else:
            places.append(len(unique))
            unique.append(x)

    def kernel(*refs):
        ins = [refs[i] for i in places]
        body(*ins, *refs[len(unique):])

    moved = sum(4 * x.size for x in unique) + sum(4 * functools.reduce(lambda a, b: a * b, s) for s in shapes)
    return pl.pallas_call(
        kernel,
        out_shape=[jax.ShapeDtypeStruct(s, jnp.float32) for s in shapes],
        in_specs=[pl.BlockSpec(memory_space=pltpu.VMEM)] * len(unique),
        out_specs=[pl.BlockSpec(memory_space=pltpu.VMEM)] * len(shapes),
        compiler_params=pltpu.CompilerParams(vmem_limit_bytes=40 * 1024 * 1024),
        cost_estimate=pl.CostEstimate(flops=flops, bytes_accessed=moved, transcendentals=0),
        name=name,
    )(*unique)


def iotas(c, d):
    return lax.broadcasted_iota(jnp.int32, (c, d), 0), lax.broadcasted_iota(jnp.int32, (c, d), 1)


def next_c(x, halo, row):
    c = x.shape[0]
    return jnp.where(row == c - 1, halo, pltpu.roll(x, c - 1, 0))


def prev_c(x, halo, row):
    return jnp.where(row == 0, halo, pltpu.roll(x, 1, 0))


def next_d(x, other, lane):
    d = x.shape[1]
    return pltpu.roll(jnp.where(lane == 0, other, x), d - 1, 1)


def prev_d(x, other, lane):
    d = x.shape[1]
    return pltpu.roll(jnp.where(lane == d - 1, other, x), 1, 1)


def prev_b(ref, halo, b):
    return jnp.where(b == 0, halo, ref[0, jnp.maximum(b - 1, 0)])


def next_b(ref, halo, b, count):
    return jnp.where(b == count - 1, halo, ref[0, jnp.minimum(b + 1, count - 1)])


def pack_d(field, low, high, lane):
    d = field.shape[1]
    return jnp.where((lane == 0) | (lane == d - 1), field, pltpu.roll(jnp.where(lane == 0, low, high), d // 2, 1))


def unpack_d(packed):
    return pltpu.roll(packed, packed.shape[1] // 2, 1)


def neighbours(ref, before_b, after_b, gz_before, gz_after, wa_before, wa_after, b, row, lane):
    count = ref.shape[1]
    x = ref[0, b]
    return [
        next_b(ref, after_b[0], b, count),
        prev_b(ref, before_b[0], b),
        next_c(x, gz_after[1, pl.ds(b, 1), :], row),
        prev_c(x, gz_before[0, pl.ds(b, 1), :], row),
        next_d(x, wa_after[0, b], lane),
        prev_d(x, wa_before[0, b], lane),
    ]


def prepare_body(pair, rates, labels, cot, start, f_ref, g_ref, w_ref, up_ref, down_ref, gz_ref, *u_refs):
    count, c, d = g_ref.shape[1:]
    row, lane = iotas(c, d)

    def step(b, _):
        r = [rates[j, 0, b] for j in range(8)]
        total = ((r[0] + r[1]) + (r[2] + r[3])) + ((r[4] + r[5]) + (r[6] + r[7]))
        f = jnp.where(labels[0, b] == 0, DAMP / total, 0.0)
        g = f * cot[0, b]
        f_ref[0, b] = f
        g_ref[0, b] = g
        if pair:
            u_refs[0][0, b] = (r[0] + r[1]) * g
        else:
            u_refs[0][0, b] = r[0] * g
            u_refs[1][0, b] = r[1] * g
        w_ref[0, b] = pack_d(start[0, b], r[7] * g, r[6] * g, lane)
        gz_ref[0, pl.ds(b, 1), :] = start[0, b, c - 1 :, :]
        gz_ref[1, pl.ds(b, 1), :] = start[0, b, :1, :]
        gz_ref[2, pl.ds(b, 1), :] = (r[4] * g)[c - 1 :]
        gz_ref[3, pl.ds(b, 1), :] = (r[5] * g)[:1]
        return 0

    lax.fori_loop(0, count, step, 0)
    up_ref[0] = start[0, count - 1]
    up_ref[1] = rates[2, 0, count - 1] * g_ref[0, count - 1]
    down_ref[0] = start[0, 0]
    down_ref[1] = rates[3, 0, 0] * g_ref[0, 0]


def forward_body(pair, rates, f_ref, labels, q, q_before, q_after, up, down, gz_before, gz_after, wa_before, wa_after, first, s_ref):
    count, c, d = q.shape[1:]
    row, lane = iotas(c, d)

    def step(b, _):
        f = f_ref[0, b]
        near = neighbours(q, up, down, gz_before, gz_after, wa_before, wa_after, b, row, lane)
        total = sum(rates[2 + k, 0, b] * near[k] for k in range(6))
        if pair:
            total = total + (rates[0, 0, b] + rates[1, 0, b]) * q_after[0, b]
        else:
            total = total + rates[0, 0, b] * q_after[0, b] + rates[1, 0, b] * q_before[0, b]
        s = f * total
        label = labels[0, b]
        s_ref[0, b] = s
        first[0, b] = jnp.where(label == 0, KEEP * q[0, b] + s, jnp.where(label == 2, 1.0, 0.0))
        return 0

    lax.fori_loop(0, count, step, 0)


def spread(rates, f_ref, x, g, up, down, gz_before, gz_after, wa_before, wa_after, at, b, row, lane):
    count, c, d = g.shape[1:]
    f, own = f_ref[0, b], g[0, b]
    below, above = jnp.maximum(b - 1, 0), jnp.minimum(b + 1, count - 1)
    out = jnp.where(f > 0.0, KEEP * x, 0.0)
    out = out + jnp.where(b == 0, up[at], rates[2, 0, below] * g[0, below])
    out = out + jnp.where(b == count - 1, down[at], rates[3, 0, above] * g[0, above])
    out = out + prev_c(rates[4, 0, b] * own, gz_before[2 * at, pl.ds(b, 1), :], row)
    out = out + next_c(rates[5, 0, b] * own, gz_after[2 * at + 1, pl.ds(b, 1), :], row)
    out = out + prev_d(rates[6, 0, b] * own, unpack_d(wa_before[0, b]), lane)
    out = out + next_d(rates[7, 0, b] * own, unpack_d(wa_after[0, b]), lane)
    return out


def back_body(pair, rates, f_ref, cot, g, u_before, u_after, up, down, gz_before, gz_after, wa_before, wa_after, first,
              back, h_ref, w_ref, up_ref, down_ref, gz_ref, *v_refs):
    count, c, d = g.shape[1:]
    row, lane = iotas(c, d)

    def step(b, _):
        out = spread(rates, f_ref, cot[0, b], g, up, down, gz_before, gz_after, wa_before, wa_after, 1, b, row, lane)
        if pair:
            out = out + u_before[0, b]
        else:
            out = out + u_before[0, b] + u_after[0, b]
        h = f_ref[0, b] * out
        back[0, b] = out
        h_ref[0, b] = h
        if pair:
            v_refs[0][0, b] = (rates[0, 0, b] + rates[1, 0, b]) * h
        else:
            v_refs[0][0, b] = rates[0, 0, b] * h
            v_refs[1][0, b] = rates[1, 0, b] * h
        w_ref[0, b] = pack_d(first[0, b], rates[7, 0, b] * h, rates[6, 0, b] * h, lane)
        gz_ref[0, pl.ds(b, 1), :] = first[0, b, c - 1 :, :]
        gz_ref[1, pl.ds(b, 1), :] = first[0, b, :1, :]
        gz_ref[2, pl.ds(b, 1), :] = (rates[4, 0, b] * h)[c - 1 :]
        gz_ref[3, pl.ds(b, 1), :] = (rates[5, 0, b] * h)[:1]
        return 0

    lax.fori_loop(0, count, step, 0)
    up_ref[0] = first[0, count - 1]
    up_ref[1] = rates[2, 0, count - 1] * h_ref[0, count - 1]
    down_ref[0] = first[0, 0]
    down_ref[1] = rates[3, 0, 0] * h_ref[0, 0]


def last_body(rates, f_ref, labels, g, h, s_ref, start, start_before, start_after, up0, down0, gz_before0, gz_after0, wa_before0,
              wa_after0, first, first_before, first_after, up1, down1, gz_before1, gz_after1, wa_before1, wa_after1, back, committor, out, partial):
    count, c, d = first.shape[1:]
    row, lane = iotas(c, d)

    def step(b, _):
        f = f_ref[0, b]
        near1 = [first_after[0, b], first_before[0, b]]
        near1 += neighbours(first, up1, down1, gz_before1, gz_after1, wa_before1, wa_after1, b, row, lane)
        s1 = f * sum(rates[k, 0, b] * near1[k] for k in range(8))
        label = labels[0, b]
        committor[0, b] = jnp.where(label == 0, KEEP * first[0, b] + s1, jnp.where(label == 2, 1.0, 0.0))
        near0 = [start_after[0, b], start_before[0, b]]
        near0 += neighbours(start, up0, down0, gz_before0, gz_after0, wa_before0, wa_after0, b, row, lane)
        avg1, avg0 = s1 * (1.0 / DAMP), s_ref[0, b] * (1.0 / DAMP)
        gb, hb = g[0, b], h[0, b]
        for k in range(8):
            out[k, 0, b] = gb * (near1[k] - avg1) + hb * (near0[k] - avg0)
        partial[0, b] = spread(rates, f_ref, back[0, b], h, up1, down1, gz_before1, gz_after1, wa_before1, wa_after1, 1, b, row, lane)
        return 0

    lax.fori_loop(0, count, step, 0)


def on_device(start, rates, labels, cotangent):
    _, b, c, d = start.shape
    block = (1, b, c, d)
    cells = b * c * d
    pair = lax.axis_size("grp") == 2
    blocks = [block] * (1 if pair else 2)
    faces = [(2, c, d), (2, c, d), (4, b, d)]

    start_before, start_after = both_ways(start, start, "grp")
    f, g, w0, up, down, gz, *u = call(
        functools.partial(prepare_body, pair), "prepare", [rates, labels, cotangent, start], [block] * 3 + faces + blocks, 20 * cells
    )
    u_before, u_after = both_ways(u[0], u[-1], "grp")
    up0, down0 = both_ways(up, down, "gy")
    gz_before0, gz_after0 = both_ways(gz, gz, "gz")
    wa0 = both_ways(w0, w0, "wa")

    first, s0 = call(
        functools.partial(forward_body, pair),
        "forward",
        [rates, f, labels, start, start_before, start_after, up0, down0, gz_before0, gz_after0, *wa0],
        [block] * 2,
        30 * cells,
    )
    first_before, first_after = both_ways(first, first, "grp")

    back, h, w1, up, down, gz, *v = call(
        functools.partial(back_body, pair),
        "backward",
        [rates, f, cotangent, g, u_before, u_after, up0, down0, gz_before0, gz_after0, *wa0, first],
        [block] * 3 + faces + blocks,
        30 * cells,
    )
    v_before, v_after = both_ways(v[0], v[-1], "grp")
    up1, down1 = both_ways(up, down, "gy")
    gz_before1, gz_after1 = both_ways(gz, gz, "gz")
    wa1 = both_ways(w1, w1, "wa")

    committor, grad_rates, grad = call(
        last_body,
        "last",
        [rates, f, labels, g, h, s0, start, start_before, start_after, up0, down0, gz_before0, gz_after0, *wa0,
         first, first_before, first_after, up1, down1, gz_before1, gz_after1, *wa1, back],
        [block, (8, 1, b, c, d), block],
        120 * cells,
    )
    grad_start = grad + v_before if pair else grad + v_before + v_after
    return committor, grad_start, grad_rates


def solution(mesh):
    placed = (
        P("grp", "gy", "gz", "wa"),
        P(None, "grp", "gy", "gz", "wa"),
        P("grp", "gy", "gz", "wa"),
        P("grp", "gy", "gz", "wa"),
    )
    return jax.shard_map(
        on_device,
        mesh=mesh,
        in_specs=placed,
        out_specs=(
            P("grp", "gy", "gz", "wa"),
            P("grp", "gy", "gz", "wa"),
            P(None, "grp", "gy", "gz", "wa"),
        ),
        check_vma=False,
    )
```

```python
import functools

import jax
import jax.numpy as jnp
from jax import lax
from jax.experimental import pallas as pl
from jax.experimental.pallas import tpu as pltpu
from jax.sharding import PartitionSpec as P

DAMP = 0.8
KEEP = 1.0 - 0.8


def ring(axis, distance):
    size = lax.axis_size(axis)
    return [(i, (i + distance) % size) for i in range(size)]


def both_ways(up, down, axis):
    if lax.axis_size(axis) == 2 and up is down:
        other = lax.ppermute(up, axis, ring(axis, 1))
        return other, other
    return lax.ppermute(up, axis, ring(axis, 1)), lax.ppermute(down, axis, ring(axis, -1))


def call(body, name, operands, shapes, flops):
    unique, places = [], []
    for x in operands:
        for i, y in enumerate(unique):
            if x is y:
                places.append(i)
                break
        else:
            places.append(len(unique))
            unique.append(x)

    def kernel(*refs):
        ins = [refs[i] for i in places]
        body(*ins, *refs[len(unique):])

    moved = sum(4 * x.size for x in unique) + sum(4 * functools.reduce(lambda a, b: a * b, s) for s in shapes)
    return pl.pallas_call(
        kernel,
        out_shape=[jax.ShapeDtypeStruct(s, jnp.float32) for s in shapes],
        in_specs=[pl.BlockSpec(memory_space=pltpu.VMEM)] * len(unique),
        out_specs=[pl.BlockSpec(memory_space=pltpu.VMEM)] * len(shapes),
        compiler_params=pltpu.CompilerParams(vmem_limit_bytes=40 * 1024 * 1024),
        cost_estimate=pl.CostEstimate(flops=flops, bytes_accessed=moved, transcendentals=0),
        name=name,
    )(*unique)


def rows(first, stop, step):
    unroll = 4 if (stop - first) % 4 == 0 else 1
    lax.fori_loop(first, stop, lambda b, _: step(b), None, unroll=unroll)


def iotas(c, d):
    return lax.broadcasted_iota(jnp.int32, (c, d), 0), lax.broadcasted_iota(jnp.int32, (c, d), 1)


def next_c(x, halo, row):
    c = x.shape[0]
    return jnp.where(row == c - 1, halo, pltpu.roll(x, c - 1, 0))


def prev_c(x, halo, row):
    return jnp.where(row == 0, halo, pltpu.roll(x, 1, 0))


def next_d(x, other, lane):
    d = x.shape[1]
    return pltpu.roll(jnp.where(lane == 0, other, x), d - 1, 1)


def prev_d(x, other, lane):
    d = x.shape[1]
    return pltpu.roll(jnp.where(lane == d - 1, other, x), 1, 1)


def prev_b(ref, halo, b):
    return jnp.where(b == 0, halo, ref[0, jnp.maximum(b - 1, 0)])


def next_b(ref, halo, b, count):
    return jnp.where(b == count - 1, halo, ref[0, jnp.minimum(b + 1, count - 1)])


def pack_d(field, low, high, lane):
    d = field.shape[1]
    return jnp.where((lane == 0) | (lane == d - 1), field, pltpu.roll(jnp.where(lane == 0, low, high), d // 2, 1))


def unpack_d(packed):
    return pltpu.roll(packed, packed.shape[1] // 2, 1)


def neighbours(ref, before_b, after_b, gz_before, gz_after, wa_before, wa_after, b, row, lane):
    count = ref.shape[1]
    x = ref[0, b]
    return [
        next_b(ref, after_b[0], b, count),
        prev_b(ref, before_b[0], b),
        next_c(x, gz_after[1, pl.ds(b, 1), :], row),
        prev_c(x, gz_before[0, pl.ds(b, 1), :], row),
        next_d(x, wa_after[0, b], lane),
        prev_d(x, wa_before[0, b], lane),
    ]


def prepare_body(pair, rates, labels, cot, start, f_ref, g_ref, w_ref, up_ref, down_ref, gz_ref, *u_refs):
    count, c, d = g_ref.shape[1:]
    row, lane = iotas(c, d)

    def step(b):
        r = [rates[j, 0, b] for j in range(8)]
        total = ((r[0] + r[1]) + (r[2] + r[3])) + ((r[4] + r[5]) + (r[6] + r[7]))
        f = jnp.where(labels[0, b] == 0, DAMP / total, 0.0)
        g = f * cot[0, b]
        f_ref[0, b] = f
        g_ref[0, b] = g
        if pair:
            u_refs[0][0, b] = (r[0] + r[1]) * g
        else:
            u_refs[0][0, b] = r[0] * g
            u_refs[1][0, b] = r[1] * g
        w_ref[0, b] = pack_d(start[0, b], r[7] * g, r[6] * g, lane)
        gz_ref[0, pl.ds(b, 1), :] = start[0, b, c - 1 :, :]
        gz_ref[1, pl.ds(b, 1), :] = start[0, b, :1, :]
        gz_ref[2, pl.ds(b, 1), :] = (r[4] * g)[c - 1 :]
        gz_ref[3, pl.ds(b, 1), :] = (r[5] * g)[:1]

    rows(0, count, step)
    up_ref[0] = start[0, count - 1]
    up_ref[1] = rates[2, 0, count - 1] * g_ref[0, count - 1]
    down_ref[0] = start[0, 0]
    down_ref[1] = rates[3, 0, 0] * g_ref[0, 0]


def forward_body(pair, rates, f_ref, labels, q, q_before, q_after, up, down, gz_before, gz_after, wa_before, wa_after, first, s_ref):
    count, c, d = q.shape[1:]
    row, lane = iotas(c, d)

    def step(b):
        f = f_ref[0, b]
        near = neighbours(q, up, down, gz_before, gz_after, wa_before, wa_after, b, row, lane)
        total = sum(rates[2 + k, 0, b] * near[k] for k in range(6))
        if pair:
            total = total + (rates[0, 0, b] + rates[1, 0, b]) * q_after[0, b]
        else:
            total = total + rates[0, 0, b] * q_after[0, b] + rates[1, 0, b] * q_before[0, b]
        s = f * total
        label = labels[0, b]
        s_ref[0, b] = s
        first[0, b] = jnp.where(label == 0, KEEP * q[0, b] + s, jnp.where(label == 2, 1.0, 0.0))

    rows(0, count, step)


def spread(rates, f_ref, x, g, up, down, gz_before, gz_after, wa_before, wa_after, at, b, row, lane):
    count, c, d = g.shape[1:]
    f, own = f_ref[0, b], g[0, b]
    below, above = jnp.maximum(b - 1, 0), jnp.minimum(b + 1, count - 1)
    out = jnp.where(f > 0.0, KEEP * x, 0.0)
    out = out + jnp.where(b == 0, up[at], rates[2, 0, below] * g[0, below])
    out = out + jnp.where(b == count - 1, down[at], rates[3, 0, above] * g[0, above])
    out = out + prev_c(rates[4, 0, b] * own, gz_before[2 * at, pl.ds(b, 1), :], row)
    out = out + next_c(rates[5, 0, b] * own, gz_after[2 * at + 1, pl.ds(b, 1), :], row)
    out = out + prev_d(rates[6, 0, b] * own, unpack_d(wa_before[0, b]), lane)
    out = out + next_d(rates[7, 0, b] * own, unpack_d(wa_after[0, b]), lane)
    return out


def back_body(pair, rates, f_ref, cot, g, u_before, u_after, up, down, gz_before, gz_after, wa_before, wa_after, first,
              back, h_ref, w_ref, up_ref, down_ref, gz_ref, *v_refs):
    count, c, d = g.shape[1:]
    row, lane = iotas(c, d)

    half = len(v_refs) // 2
    cut = v_refs[0].shape[1]

    def step(b, v, shift):
        out = spread(rates, f_ref, cot[0, b], g, up, down, gz_before, gz_after, wa_before, wa_after, 1, b, row, lane)
        if pair:
            out = out + u_before[0, b]
        else:
            out = out + u_before[0, b] + u_after[0, b]
        h = f_ref[0, b] * out
        back[0, b] = out
        h_ref[0, b] = h
        if pair:
            v[0][0, b - shift] = (rates[0, 0, b] + rates[1, 0, b]) * h
        else:
            v[0][0, b - shift] = rates[0, 0, b] * h
            v[1][0, b - shift] = rates[1, 0, b] * h
        w_ref[0, b] = pack_d(first[0, b], rates[7, 0, b] * h, rates[6, 0, b] * h, lane)
        gz_ref[0, pl.ds(b, 1), :] = first[0, b, c - 1 :, :]
        gz_ref[1, pl.ds(b, 1), :] = first[0, b, :1, :]
        gz_ref[2, pl.ds(b, 1), :] = (rates[4, 0, b] * h)[c - 1 :]
        gz_ref[3, pl.ds(b, 1), :] = (rates[5, 0, b] * h)[:1]

    rows(0, cut, lambda b: step(b, v_refs[:half], 0))
    rows(cut, count, lambda b: step(b, v_refs[half:], cut))
    up_ref[0] = first[0, count - 1]
    up_ref[1] = rates[2, 0, count - 1] * h_ref[0, count - 1]
    down_ref[0] = first[0, 0]
    down_ref[1] = rates[3, 0, 0] * h_ref[0, 0]


def last_body(rates, f_ref, labels, g, h, s_ref, start, start_before, start_after, up0, down0, gz_before0, gz_after0, wa_before0,
              wa_after0, first, first_before, first_after, up1, down1, gz_before1, gz_after1, wa_before1, wa_after1, back, committor, out, partial):
    count, c, d = first.shape[1:]
    row, lane = iotas(c, d)

    def step(b):
        f = f_ref[0, b]
        near1 = [first_after[0, b], first_before[0, b]]
        near1 += neighbours(first, up1, down1, gz_before1, gz_after1, wa_before1, wa_after1, b, row, lane)
        s1 = f * sum(rates[k, 0, b] * near1[k] for k in range(8))
        label = labels[0, b]
        committor[0, b] = jnp.where(label == 0, KEEP * first[0, b] + s1, jnp.where(label == 2, 1.0, 0.0))
        near0 = [start_after[0, b], start_before[0, b]]
        near0 += neighbours(start, up0, down0, gz_before0, gz_after0, wa_before0, wa_after0, b, row, lane)
        avg1, avg0 = s1 * (1.0 / DAMP), s_ref[0, b] * (1.0 / DAMP)
        gb, hb = g[0, b], h[0, b]
        for k in range(8):
            out[k, 0, b] = gb * (near1[k] - avg1) + hb * (near0[k] - avg0)
        partial[0, b] = spread(rates, f_ref, back[0, b], h, up1, down1, gz_before1, gz_after1, wa_before1, wa_after1, 1, b, row, lane)

    rows(0, count, step)


def finish(done, grad, came, first):
    parts = [came[0]] if came[0] is came[1] else list(came)
    shape = came[0].shape

    def kernel(*refs):
        given, refs = refs[: done is not None], refs[done is not None :]
        grad_ref, came_refs, (out, total, sem) = refs[0], refs[1:-3], refs[-3:]
        acc = grad_ref[0, first : first + shape[1]]
        for ref in came_refs:
            acc = acc + ref[0]
        total[...] = acc
        copy = pltpu.make_async_copy(total, out.at[0, pl.ds(first, shape[1])], sem)
        copy.start()
        copy.wait()

    given = [] if done is None else [done]
    return pl.pallas_call(
        kernel,
        out_shape=jax.ShapeDtypeStruct(grad.shape, jnp.float32),
        in_specs=[pl.BlockSpec(memory_space=pl.ANY)] * len(given) + [pl.BlockSpec(memory_space=pltpu.VMEM)] * (1 + len(parts)),
        out_specs=pl.BlockSpec(memory_space=pl.ANY),
        scratch_shapes=[pltpu.VMEM(shape[1:], jnp.float32), pltpu.SemaphoreType.DMA],
        input_output_aliases={0: 0} if given else {},
        name="finish",
    )(*given, grad, *parts)


def on_device(start, rates, labels, cotangent):
    _, b, c, d = start.shape
    block = (1, b, c, d)
    cells = b * c * d
    pair = lax.axis_size("grp") == 2
    blocks = [block] * (1 if pair else 2)
    tail = max(1, b // 6)
    faces = [(2, c, d), (2, c, d), (4, b, d)]

    start_before, start_after = both_ways(start, start, "grp")
    f, g, w0, up, down, gz, *u = call(
        functools.partial(prepare_body, pair), "prepare", [rates, labels, cotangent, start], [block] * 3 + faces + blocks, 20 * cells
    )
    u_before, u_after = both_ways(u[0], u[-1], "grp")
    up0, down0 = both_ways(up, down, "gy")
    gz_before0, gz_after0 = both_ways(gz, gz, "gz")
    wa0 = both_ways(w0, w0, "wa")

    first, s0 = call(
        functools.partial(forward_body, pair),
        "forward",
        [rates, f, labels, start, start_before, start_after, up0, down0, gz_before0, gz_after0, *wa0],
        [block] * 2,
        30 * cells,
    )
    first_before, first_after = both_ways(first, first, "grp")

    back, h, w1, up, down, gz, *v = call(
        functools.partial(back_body, pair),
        "backward",
        [rates, f, cotangent, g, u_before, u_after, up0, down0, gz_before0, gz_after0, *wa0, first],
        [block] * 3 + faces + [(1, b - tail, c, d)] * len(blocks) + [(1, tail, c, d)] * len(blocks),
        30 * cells,
    )
    most = both_ways(v[0], v[len(blocks) - 1], "grp")
    rest = both_ways(v[len(blocks)], v[-1], "grp")
    up1, down1 = both_ways(up, down, "gy")
    gz_before1, gz_after1 = both_ways(gz, gz, "gz")
    wa1 = both_ways(w1, w1, "wa")

    committor, grad_rates, grad = call(
        last_body,
        "last",
        [rates, f, labels, g, h, s0, start, start_before, start_after, up0, down0, gz_before0, gz_after0, *wa0,
         first, first_before, first_after, up1, down1, gz_before1, gz_after1, *wa1, back],
        [block, (8, 1, b, c, d), block],
        120 * cells,
    )
    grad_start = finish(finish(None, grad, most, 0), grad, rest, b - tail)
    return committor, grad_start, grad_rates


def solution(mesh):
    placed = (
        P("grp", "gy", "gz", "wa"),
        P(None, "grp", "gy", "gz", "wa"),
        P("grp", "gy", "gz", "wa"),
        P("grp", "gy", "gz", "wa"),
    )
    return jax.shard_map(
        on_device,
        mesh=mesh,
        in_specs=placed,
        out_specs=(
            P("grp", "gy", "gz", "wa"),
            P("grp", "gy", "gz", "wa"),
            P(None, "grp", "gy", "gz", "wa"),
        ),
        check_vma=False,
    )
```

```python
import functools

import jax
import jax.numpy as jnp
from jax import lax
from jax.experimental import pallas as pl
from jax.experimental.pallas import tpu as pltpu
from jax.sharding import PartitionSpec as P

DAMP = 0.8
KEEP = 1.0 - 0.8


def ring(axis, distance):
    size = lax.axis_size(axis)
    return [(i, (i + distance) % size) for i in range(size)]


def both_ways(up, down, axis):
    if lax.axis_size(axis) == 2 and up is down:
        other = lax.ppermute(up, axis, ring(axis, 1))
        return other, other
    return lax.ppermute(up, axis, ring(axis, 1)), lax.ppermute(down, axis, ring(axis, -1))


def call(body, name, operands, shapes, flops):
    unique, places = [], []
    for x in operands:
        for i, y in enumerate(unique):
            if x is y:
                places.append(i)
                break
        else:
            places.append(len(unique))
            unique.append(x)

    def kernel(*refs):
        ins = [refs[i] for i in places]
        body(*ins, *refs[len(unique):])

    moved = sum(4 * x.size for x in unique) + sum(4 * functools.reduce(lambda a, b: a * b, s) for s in shapes)
    return pl.pallas_call(
        kernel,
        out_shape=[jax.ShapeDtypeStruct(s, jnp.float32) for s in shapes],
        in_specs=[pl.BlockSpec(memory_space=pltpu.VMEM)] * len(unique),
        out_specs=[pl.BlockSpec(memory_space=pltpu.VMEM)] * len(shapes),
        compiler_params=pltpu.CompilerParams(vmem_limit_bytes=40 * 1024 * 1024),
        cost_estimate=pl.CostEstimate(flops=flops, bytes_accessed=moved, transcendentals=0),
        name=name,
    )(*unique)


def rows(first, stop, step):
    unroll = 4 if (stop - first) % 4 == 0 else 1
    lax.fori_loop(first, stop, lambda b, _: step(b), None, unroll=unroll)


def iotas(c, d):
    return lax.broadcasted_iota(jnp.int32, (c, d), 0), lax.broadcasted_iota(jnp.int32, (c, d), 1)


def next_c(x, halo, row):
    c = x.shape[0]
    return jnp.where(row == c - 1, halo, pltpu.roll(x, c - 1, 0))


def prev_c(x, halo, row):
    return jnp.where(row == 0, halo, pltpu.roll(x, 1, 0))


def next_d(x, other, lane):
    d = x.shape[1]
    return pltpu.roll(jnp.where(lane == 0, other, x), d - 1, 1)


def prev_d(x, other, lane):
    d = x.shape[1]
    return pltpu.roll(jnp.where(lane == d - 1, other, x), 1, 1)


def prev_b(ref, halo, b):
    return jnp.where(b == 0, halo, ref[0, jnp.maximum(b - 1, 0)])


def next_b(ref, halo, b, count):
    return jnp.where(b == count - 1, halo, ref[0, jnp.minimum(b + 1, count - 1)])


def pack_d(field, low, high, lane):
    d = field.shape[1]
    return jnp.where((lane == 0) | (lane == d - 1), field, pltpu.roll(jnp.where(lane == 0, low, high), d // 2, 1))


def unpack_d(packed):
    return pltpu.roll(packed, packed.shape[1] // 2, 1)


def neighbours(ref, before_b, after_b, gz_before, gz_after, wa_before, wa_after, b, row, lane):
    count = ref.shape[1]
    x = ref[0, b]
    return [
        next_b(ref, after_b[0], b, count),
        prev_b(ref, before_b[0], b),
        next_c(x, gz_after[1, pl.ds(b, 1), :], row),
        prev_c(x, gz_before[0, pl.ds(b, 1), :], row),
        next_d(x, wa_after[0, b], lane),
        prev_d(x, wa_before[0, b], lane),
    ]


def prepare_body(pair, rates, labels, cot, start, f_ref, g_ref, w_ref, up_ref, down_ref, gz_ref, *u_refs):
    count, c, d = g_ref.shape[1:]
    row, lane = iotas(c, d)

    def step(b):
        r = [rates[j, 0, b] for j in range(8)]
        total = ((r[0] + r[1]) + (r[2] + r[3])) + ((r[4] + r[5]) + (r[6] + r[7]))
        f = jnp.where(labels[0, b] == 0, DAMP / total, 0.0)
        g = f * cot[0, b]
        f_ref[0, b] = f
        g_ref[0, b] = g
        if pair:
            u_refs[0][0, b] = (r[0] + r[1]) * g
        else:
            u_refs[0][0, b] = r[0] * g
            u_refs[1][0, b] = r[1] * g
        w_ref[0, b] = pack_d(start[0, b], r[7] * g, r[6] * g, lane)
        gz_ref[0, pl.ds(b, 1), :] = start[0, b, c - 1 :, :]
        gz_ref[1, pl.ds(b, 1), :] = start[0, b, :1, :]
        gz_ref[2, pl.ds(b, 1), :] = (r[4] * g)[c - 1 :]
        gz_ref[3, pl.ds(b, 1), :] = (r[5] * g)[:1]

    rows(0, count, step)
    up_ref[0] = start[0, count - 1]
    up_ref[1] = rates[2, 0, count - 1] * g_ref[0, count - 1]
    down_ref[0] = start[0, 0]
    down_ref[1] = rates[3, 0, 0] * g_ref[0, 0]


def forward_body(pair, rates, f_ref, labels, q, q_before, q_after, up, down, gz_before, gz_after, wa_before, wa_after, first, s_ref):
    count, c, d = q.shape[1:]
    row, lane = iotas(c, d)

    def step(b):
        f = f_ref[0, b]
        near = neighbours(q, up, down, gz_before, gz_after, wa_before, wa_after, b, row, lane)
        total = sum(rates[2 + k, 0, b] * near[k] for k in range(6))
        if pair:
            total = total + (rates[0, 0, b] + rates[1, 0, b]) * q_after[0, b]
        else:
            total = total + rates[0, 0, b] * q_after[0, b] + rates[1, 0, b] * q_before[0, b]
        s = f * total
        label = labels[0, b]
        s_ref[0, b] = s
        first[0, b] = jnp.where(label == 0, KEEP * q[0, b] + s, jnp.where(label == 2, 1.0, 0.0))

    rows(0, count, step)


def spread(rates, f_ref, x, g, up, down, gz_before, gz_after, wa_before, wa_after, at, b, row, lane):
    count, c, d = g.shape[1:]
    f, own = f_ref[0, b], g[0, b]
    below, above = jnp.maximum(b - 1, 0), jnp.minimum(b + 1, count - 1)
    out = jnp.where(f > 0.0, KEEP * x, 0.0)
    out = out + jnp.where(b == 0, up[at], rates[2, 0, below] * g[0, below])
    out = out + jnp.where(b == count - 1, down[at], rates[3, 0, above] * g[0, above])
    out = out + prev_c(rates[4, 0, b] * own, gz_before[2 * at, pl.ds(b, 1), :], row)
    out = out + next_c(rates[5, 0, b] * own, gz_after[2 * at + 1, pl.ds(b, 1), :], row)
    out = out + prev_d(rates[6, 0, b] * own, unpack_d(wa_before[0, b]), lane)
    out = out + next_d(rates[7, 0, b] * own, unpack_d(wa_after[0, b]), lane)
    return out


def back_body(pair, rates, f_ref, cot, g, u_before, u_after, up, down, gz_before, gz_after, wa_before, wa_after, first,
              back, h_ref, w_ref, up_ref, down_ref, gz_ref, *v_refs):
    count, c, d = g.shape[1:]
    row, lane = iotas(c, d)

    half = len(v_refs) // 2
    cut = v_refs[0].shape[1]

    def step(b, v, shift):
        out = spread(rates, f_ref, cot[0, b], g, up, down, gz_before, gz_after, wa_before, wa_after, 1, b, row, lane)
        if pair:
            out = out + u_before[0, b]
        else:
            out = out + u_before[0, b] + u_after[0, b]
        h = f_ref[0, b] * out
        back[0, b] = out
        h_ref[0, b] = h
        if pair:
            v[0][0, b - shift] = (rates[0, 0, b] + rates[1, 0, b]) * h
        else:
            v[0][0, b - shift] = rates[0, 0, b] * h
            v[1][0, b - shift] = rates[1, 0, b] * h
        w_ref[0, b] = pack_d(first[0, b], rates[7, 0, b] * h, rates[6, 0, b] * h, lane)
        gz_ref[0, pl.ds(b, 1), :] = first[0, b, c - 1 :, :]
        gz_ref[1, pl.ds(b, 1), :] = first[0, b, :1, :]
        gz_ref[2, pl.ds(b, 1), :] = (rates[4, 0, b] * h)[c - 1 :]
        gz_ref[3, pl.ds(b, 1), :] = (rates[5, 0, b] * h)[:1]

    rows(0, cut, lambda b: step(b, v_refs[:half], 0))
    rows(cut, count, lambda b: step(b, v_refs[half:], cut))
    up_ref[0] = first[0, count - 1]
    up_ref[1] = rates[2, 0, count - 1] * h_ref[0, count - 1]
    down_ref[0] = first[0, 0]
    down_ref[1] = rates[3, 0, 0] * h_ref[0, 0]


def last_body(rates, f_ref, labels, g, h, s_ref, start, start_before, start_after, up0, down0, gz_before0, gz_after0, wa_before0,
              wa_after0, first, first_before, first_after, up1, down1, gz_before1, gz_after1, wa_before1, wa_after1, back, committor, out, partial):
    count, c, d = first.shape[1:]
    row, lane = iotas(c, d)

    def step(b):
        f = f_ref[0, b]
        near1 = [first_after[0, b], first_before[0, b]]
        near1 += neighbours(first, up1, down1, gz_before1, gz_after1, wa_before1, wa_after1, b, row, lane)
        s1 = f * sum(rates[k, 0, b] * near1[k] for k in range(8))
        label = labels[0, b]
        committor[0, b] = jnp.where(label == 0, KEEP * first[0, b] + s1, jnp.where(label == 2, 1.0, 0.0))
        near0 = [start_after[0, b], start_before[0, b]]
        near0 += neighbours(start, up0, down0, gz_before0, gz_after0, wa_before0, wa_after0, b, row, lane)
        avg1, avg0 = s1 * (1.0 / DAMP), s_ref[0, b] * (1.0 / DAMP)
        gb, hb = g[0, b], h[0, b]
        for k in range(8):
            out[k, 0, b] = gb * (near1[k] - avg1) + hb * (near0[k] - avg0)
        partial[0, b] = spread(rates, f_ref, back[0, b], h, up1, down1, gz_before1, gz_after1, wa_before1, wa_after1, 1, b, row, lane)

    rows(0, count, step)


def finish(done, grad, came, first):
    parts = [came[0]] if came[0] is came[1] else list(came)
    shape = came[0].shape

    def kernel(*refs):
        given, refs = refs[: done is not None], refs[done is not None :]
        grad_ref, came_refs, (out, total, sem) = refs[0], refs[1:-3], refs[-3:]
        acc = grad_ref[0, first : first + shape[1]]
        for ref in came_refs:
            acc = acc + ref[0]
        total[...] = acc
        copy = pltpu.make_async_copy(total, out.at[0, pl.ds(first, shape[1])], sem)
        copy.start()
        copy.wait()

    given = [] if done is None else [done]
    return pl.pallas_call(
        kernel,
        out_shape=jax.ShapeDtypeStruct(grad.shape, jnp.float32),
        in_specs=[pl.BlockSpec(memory_space=pl.ANY)] * len(given) + [pl.BlockSpec(memory_space=pltpu.VMEM)] * (1 + len(parts)),
        out_specs=pl.BlockSpec(memory_space=pl.ANY),
        scratch_shapes=[pltpu.VMEM(shape[1:], jnp.float32), pltpu.SemaphoreType.DMA],
        input_output_aliases={0: 0} if given else {},
        compiler_params=pltpu.CompilerParams(vmem_limit_bytes=4 * 1024 * 1024),
        name="finish",
    )(*given, grad, *parts)


def on_device(start, rates, labels, cotangent):
    _, b, c, d = start.shape
    block = (1, b, c, d)
    cells = b * c * d
    pair = lax.axis_size("grp") == 2
    blocks = [block] * (1 if pair else 2)
    tail = max(1, b // 6)
    faces = [(2, c, d), (2, c, d), (4, b, d)]

    start_before, start_after = both_ways(start, start, "grp")
    f, g, w0, up, down, gz, *u = call(
        functools.partial(prepare_body, pair), "prepare", [rates, labels, cotangent, start], [block] * 3 + faces + blocks, 20 * cells
    )
    u_before, u_after = both_ways(u[0], u[-1], "grp")
    up0, down0 = both_ways(up, down, "gy")
    gz_before0, gz_after0 = both_ways(gz, gz, "gz")
    wa0 = both_ways(w0, w0, "wa")

    first, s0 = call(
        functools.partial(forward_body, pair),
        "forward",
        [rates, f, labels, start, start_before, start_after, up0, down0, gz_before0, gz_after0, *wa0],
        [block] * 2,
        30 * cells,
    )
    first_before, first_after = both_ways(first, first, "grp")

    back, h, w1, up, down, gz, *v = call(
        functools.partial(back_body, pair),
        "backward",
        [rates, f, cotangent, g, u_before, u_after, up0, down0, gz_before0, gz_after0, *wa0, first],
        [block] * 3 + faces + [(1, b - tail, c, d)] * len(blocks) + [(1, tail, c, d)] * len(blocks),
        30 * cells,
    )
    most = both_ways(v[0], v[len(blocks) - 1], "grp")
    rest = both_ways(v[len(blocks)], v[-1], "grp")
    up1, down1 = both_ways(up, down, "gy")
    gz_before1, gz_after1 = both_ways(gz, gz, "gz")
    wa1 = both_ways(w1, w1, "wa")

    committor, grad_rates, grad = call(
        last_body,
        "last",
        [rates, f, labels, g, h, s0, start, start_before, start_after, up0, down0, gz_before0, gz_after0, *wa0,
         first, first_before, first_after, up1, down1, gz_before1, gz_after1, *wa1, back],
        [block, (8, 1, b, c, d), block],
        120 * cells,
    )
    grad_start = finish(finish(None, grad, most, 0), grad, rest, b - tail)
    return committor, grad_start, grad_rates


def solution(mesh):
    placed = (
        P("grp", "gy", "gz", "wa"),
        P(None, "grp", "gy", "gz", "wa"),
        P("grp", "gy", "gz", "wa"),
        P("grp", "gy", "gz", "wa"),
    )
    return jax.shard_map(
        on_device,
        mesh=mesh,
        in_specs=placed,
        out_specs=(
            P("grp", "gy", "gz", "wa"),
            P("grp", "gy", "gz", "wa"),
            P(None, "grp", "gy", "gz", "wa"),
        ),
        check_vma=False,
    )
```

```python
import functools

import jax
import jax.numpy as jnp
from jax import lax
from jax.experimental import pallas as pl
from jax.experimental.pallas import tpu as pltpu
from jax.sharding import PartitionSpec as P

DAMP = 0.8
KEEP = 1.0 - 0.8


def ring(axis, distance):
    size = lax.axis_size(axis)
    return [(i, (i + distance) % size) for i in range(size)]


def both_ways(up, down, axis):
    if lax.axis_size(axis) == 2 and up is down:
        other = lax.ppermute(up, axis, ring(axis, 1))
        return other, other
    return lax.ppermute(up, axis, ring(axis, 1)), lax.ppermute(down, axis, ring(axis, -1))


def call(body, name, operands, shapes, flops):
    unique, places = [], []
    for x in operands:
        for i, y in enumerate(unique):
            if x is y:
                places.append(i)
                break
        else:
            places.append(len(unique))
            unique.append(x)

    def kernel(*refs):
        ins = [refs[i] for i in places]
        body(*ins, *refs[len(unique):])

    moved = sum(4 * x.size for x in unique) + sum(4 * functools.reduce(lambda a, b: a * b, s) for s in shapes)
    return pl.pallas_call(
        kernel,
        out_shape=[jax.ShapeDtypeStruct(s, jnp.float32) for s in shapes],
        in_specs=[pl.BlockSpec(memory_space=pltpu.VMEM)] * len(unique),
        out_specs=[pl.BlockSpec(memory_space=pltpu.VMEM)] * len(shapes),
        compiler_params=pltpu.CompilerParams(vmem_limit_bytes=40 * 1024 * 1024),
        cost_estimate=pl.CostEstimate(flops=flops, bytes_accessed=moved, transcendentals=0),
        name=name,
    )(*unique)


def rows(first, stop, step):
    unroll = 4 if (stop - first) % 4 == 0 else 1
    lax.fori_loop(first, stop, lambda b, _: step(b), None, unroll=unroll)


def iotas(c, d):
    return lax.broadcasted_iota(jnp.int32, (c, d), 0), lax.broadcasted_iota(jnp.int32, (c, d), 1)


def next_c(x, halo, row):
    c = x.shape[0]
    return jnp.where(row == c - 1, halo, pltpu.roll(x, c - 1, 0))


def prev_c(x, halo, row):
    return jnp.where(row == 0, halo, pltpu.roll(x, 1, 0))


def next_d(x, other, lane):
    d = x.shape[1]
    return pltpu.roll(jnp.where(lane == 0, other, x), d - 1, 1)


def prev_d(x, other, lane):
    d = x.shape[1]
    return pltpu.roll(jnp.where(lane == d - 1, other, x), 1, 1)


def prev_b(ref, halo, b):
    return jnp.where(b == 0, halo, ref[0, jnp.maximum(b - 1, 0)])


def next_b(ref, halo, b, count):
    return jnp.where(b == count - 1, halo, ref[0, jnp.minimum(b + 1, count - 1)])


def pack_d(field, low, high, lane):
    d = field.shape[1]
    return jnp.where((lane == 0) | (lane == d - 1), field, pltpu.roll(jnp.where(lane == 0, low, high), d // 2, 1))


def unpack_d(packed):
    return pltpu.roll(packed, packed.shape[1] // 2, 1)


def neighbours(ref, before_b, after_b, gz_before, gz_after, wa_before, wa_after, b, row, lane):
    count = ref.shape[1]
    x = ref[0, b]
    return [
        next_b(ref, after_b[0], b, count),
        prev_b(ref, before_b[0], b),
        next_c(x, gz_after[1, pl.ds(b, 1), :], row),
        prev_c(x, gz_before[0, pl.ds(b, 1), :], row),
        next_d(x, wa_after[0, b], lane),
        prev_d(x, wa_before[0, b], lane),
    ]


def prepare_body(pair, rates, labels, cot, start, f_ref, g_ref, w_ref, up_ref, down_ref, gz_ref, *u_refs):
    count, c, d = g_ref.shape[1:]
    row, lane = iotas(c, d)

    def step(b):
        r = [rates[j, 0, b] for j in range(8)]
        total = ((r[0] + r[1]) + (r[2] + r[3])) + ((r[4] + r[5]) + (r[6] + r[7]))
        f = jnp.where(labels[0, b] == 0, DAMP / total, 0.0)
        g = f * cot[0, b]
        f_ref[0, b] = f
        g_ref[0, b] = g
        if pair:
            u_refs[0][0, b] = (r[0] + r[1]) * g
        else:
            u_refs[0][0, b] = r[0] * g
            u_refs[1][0, b] = r[1] * g
        w_ref[0, b] = pack_d(start[0, b], r[7] * g, r[6] * g, lane)
        gz_ref[0, pl.ds(b, 1), :] = start[0, b, c - 1 :, :]
        gz_ref[1, pl.ds(b, 1), :] = start[0, b, :1, :]
        gz_ref[2, pl.ds(b, 1), :] = (r[4] * g)[c - 1 :]
        gz_ref[3, pl.ds(b, 1), :] = (r[5] * g)[:1]

    rows(0, count, step)
    up_ref[0] = start[0, count - 1]
    up_ref[1] = rates[2, 0, count - 1] * g_ref[0, count - 1]
    down_ref[0] = start[0, 0]
    down_ref[1] = rates[3, 0, 0] * g_ref[0, 0]


def forward_body(pair, rates, f_ref, labels, q, q_before, q_after, up, down, gz_before, gz_after, wa_before, wa_after, first, s_ref):
    count, c, d = q.shape[1:]
    row, lane = iotas(c, d)

    def step(b):
        f = f_ref[0, b]
        near = neighbours(q, up, down, gz_before, gz_after, wa_before, wa_after, b, row, lane)
        total = sum(rates[2 + k, 0, b] * near[k] for k in range(6))
        if pair:
            total = total + (rates[0, 0, b] + rates[1, 0, b]) * q_after[0, b]
        else:
            total = total + rates[0, 0, b] * q_after[0, b] + rates[1, 0, b] * q_before[0, b]
        s = f * total
        label = labels[0, b]
        s_ref[0, b] = s
        first[0, b] = jnp.where(label == 0, KEEP * q[0, b] + s, jnp.where(label == 2, 1.0, 0.0))

    rows(0, count, step)


def spread(rates, f_ref, x, g, up, down, gz_before, gz_after, wa_before, wa_after, at, b, row, lane):
    count, c, d = g.shape[1:]
    f, own = f_ref[0, b], g[0, b]
    below, above = jnp.maximum(b - 1, 0), jnp.minimum(b + 1, count - 1)
    out = jnp.where(f > 0.0, KEEP * x, 0.0)
    out = out + jnp.where(b == 0, up[at], rates[2, 0, below] * g[0, below])
    out = out + jnp.where(b == count - 1, down[at], rates[3, 0, above] * g[0, above])
    out = out + prev_c(rates[4, 0, b] * own, gz_before[2 * at, pl.ds(b, 1), :], row)
    out = out + next_c(rates[5, 0, b] * own, gz_after[2 * at + 1, pl.ds(b, 1), :], row)
    out = out + prev_d(rates[6, 0, b] * own, unpack_d(wa_before[0, b]), lane)
    out = out + next_d(rates[7, 0, b] * own, unpack_d(wa_after[0, b]), lane)
    return out


def back_body(pair, rates, f_ref, cot, g, u_before, u_after, up, down, gz_before, gz_after, wa_before, wa_after, first,
              back, h_ref, w_ref, up_ref, down_ref, gz_ref, *v_refs):
    count, c, d = g.shape[1:]
    row, lane = iotas(c, d)

    half = len(v_refs) // 2
    cut = v_refs[0].shape[1]

    def step(b, v, shift):
        out = spread(rates, f_ref, cot[0, b], g, up, down, gz_before, gz_after, wa_before, wa_after, 1, b, row, lane)
        if pair:
            out = out + u_before[0, b]
        else:
            out = out + u_before[0, b] + u_after[0, b]
        h = f_ref[0, b] * out
        back[0, b] = out
        h_ref[0, b] = h
        if pair:
            v[0][0, b - shift] = (rates[0, 0, b] + rates[1, 0, b]) * h
        else:
            v[0][0, b - shift] = rates[0, 0, b] * h
            v[1][0, b - shift] = rates[1, 0, b] * h
        w_ref[0, b] = pack_d(first[0, b], rates[7, 0, b] * h, rates[6, 0, b] * h, lane)
        gz_ref[0, pl.ds(b, 1), :] = first[0, b, c - 1 :, :]
        gz_ref[1, pl.ds(b, 1), :] = first[0, b, :1, :]
        gz_ref[2, pl.ds(b, 1), :] = (rates[4, 0, b] * h)[c - 1 :]
        gz_ref[3, pl.ds(b, 1), :] = (rates[5, 0, b] * h)[:1]

    rows(0, cut, lambda b: step(b, v_refs[:half], 0))
    rows(cut, count, lambda b: step(b, v_refs[half:], cut))
    up_ref[0] = first[0, count - 1]
    up_ref[1] = rates[2, 0, count - 1] * h_ref[0, count - 1]
    down_ref[0] = first[0, 0]
    down_ref[1] = rates[3, 0, 0] * h_ref[0, 0]


def last_body(rates, f_ref, labels, g, h, s_ref, start, start_before, start_after, up0, down0, gz_before0, gz_after0, wa_before0,
              wa_after0, first, first_before, first_after, up1, down1, gz_before1, gz_after1, wa_before1, wa_after1, back, committor, out, partial):
    count, c, d = first.shape[1:]
    row, lane = iotas(c, d)

    def step(b):
        f = f_ref[0, b]
        near1 = [first_after[0, b], first_before[0, b]]
        near1 += neighbours(first, up1, down1, gz_before1, gz_after1, wa_before1, wa_after1, b, row, lane)
        s1 = f * sum(rates[k, 0, b] * near1[k] for k in range(8))
        label = labels[0, b]
        committor[0, b] = jnp.where(label == 0, KEEP * first[0, b] + s1, jnp.where(label == 2, 1.0, 0.0))
        near0 = [start_after[0, b], start_before[0, b]]
        near0 += neighbours(start, up0, down0, gz_before0, gz_after0, wa_before0, wa_after0, b, row, lane)
        avg1, avg0 = s1 * (1.0 / DAMP), s_ref[0, b] * (1.0 / DAMP)
        gb, hb = g[0, b], h[0, b]
        for k in range(8):
            out[k, 0, b] = gb * (near1[k] - avg1) + hb * (near0[k] - avg0)
        partial[0, b] = spread(rates, f_ref, back[0, b], h, up1, down1, gz_before1, gz_after1, wa_before1, wa_after1, 1, b, row, lane)

    rows(0, count, step)


def finish(grad, came):
    parts = [came[0]] if came[0] is came[1] else list(came)
    shape = came[0].shape

    def kernel(*refs):
        grad_ref, came_refs, (out, total, sem) = refs[0], refs[1:-3], refs[-3:]
        acc = grad_ref[0, : shape[1]]
        for ref in came_refs:
            acc = acc + ref[0]
        total[...] = acc
        copy = pltpu.make_async_copy(total, out.at[0, pl.ds(0, shape[1])], sem)
        copy.start()
        copy.wait()

    return pl.pallas_call(
        kernel,
        out_shape=jax.ShapeDtypeStruct(grad.shape, jnp.float32),
        in_specs=[pl.BlockSpec(memory_space=pltpu.VMEM)] * (1 + len(parts)),
        out_specs=pl.BlockSpec(memory_space=pl.ANY),
        scratch_shapes=[pltpu.VMEM(shape[1:], jnp.float32), pltpu.SemaphoreType.DMA],
        compiler_params=pltpu.CompilerParams(vmem_limit_bytes=4 * 1024 * 1024),
        name="finish",
    )(grad, *parts)


def on_device(start, rates, labels, cotangent):
    _, b, c, d = start.shape
    block = (1, b, c, d)
    cells = b * c * d
    pair = lax.axis_size("grp") == 2
    blocks = [block] * (1 if pair else 2)
    tail = max(1, b // 6)
    faces = [(2, c, d), (2, c, d), (4, b, d)]

    start_before, start_after = both_ways(start, start, "grp")
    f, g, w0, up, down, gz, *u = call(
        functools.partial(prepare_body, pair), "prepare", [rates, labels, cotangent, start], [block] * 3 + faces + blocks, 20 * cells
    )
    u_before, u_after = both_ways(u[0], u[-1], "grp")
    up0, down0 = both_ways(up, down, "gy")
    gz_before0, gz_after0 = both_ways(gz, gz, "gz")
    wa0 = both_ways(w0, w0, "wa")

    first, s0 = call(
        functools.partial(forward_body, pair),
        "forward",
        [rates, f, labels, start, start_before, start_after, up0, down0, gz_before0, gz_after0, *wa0],
        [block] * 2,
        30 * cells,
    )
    first_before, first_after = both_ways(first, first, "grp")

    back, h, w1, up, down, gz, *v = call(
        functools.partial(back_body, pair),
        "backward",
        [rates, f, cotangent, g, u_before, u_after, up0, down0, gz_before0, gz_after0, *wa0, first],
        [block] * 3 + faces + [(1, b - tail, c, d)] * len(blocks) + [(1, tail, c, d)] * len(blocks),
        30 * cells,
    )
    most = both_ways(v[0], v[len(blocks) - 1], "grp")
    rest = both_ways(v[len(blocks)], v[-1], "grp")
    up1, down1 = both_ways(up, down, "gy")
    gz_before1, gz_after1 = both_ways(gz, gz, "gz")
    wa1 = both_ways(w1, w1, "wa")

    committor, grad_rates, grad = call(
        last_body,
        "last",
        [rates, f, labels, g, h, s0, start, start_before, start_after, up0, down0, gz_before0, gz_after0, *wa0,
         first, first_before, first_after, up1, down1, gz_before1, gz_after1, *wa1, back],
        [block, (8, 1, b, c, d), block],
        120 * cells,
    )
    last_rows = grad[:, b - tail :] + rest[0]
    if not pair:
        last_rows = last_rows + rest[1]
    grad_start = lax.dynamic_update_slice(finish(grad, most), last_rows, (0, b - tail, 0, 0))
    return committor, grad_start, grad_rates


def solution(mesh):
    placed = (
        P("grp", "gy", "gz", "wa"),
        P(None, "grp", "gy", "gz", "wa"),
        P("grp", "gy", "gz", "wa"),
        P("grp", "gy", "gz", "wa"),
    )
    return jax.shard_map(
        on_device,
        mesh=mesh,
        in_specs=placed,
        out_specs=(
            P("grp", "gy", "gz", "wa"),
            P("grp", "gy", "gz", "wa"),
            P(None, "grp", "gy", "gz", "wa"),
        ),
        check_vma=False,
    )
```

```python
import functools

import jax
import jax.numpy as jnp
from jax import lax
from jax.experimental import pallas as pl
from jax.experimental.pallas import tpu as pltpu
from jax.sharding import PartitionSpec as P

DAMP = 0.8
KEEP = 1.0 - 0.8


def ring(axis, distance):
    size = lax.axis_size(axis)
    return [(i, (i + distance) % size) for i in range(size)]


def both_ways(up, down, axis):
    if lax.axis_size(axis) == 2 and up is down:
        other = lax.ppermute(up, axis, ring(axis, 1))
        return other, other
    return lax.ppermute(up, axis, ring(axis, 1)), lax.ppermute(down, axis, ring(axis, -1))


def row_swap(row):
    ys, zs = lax.axis_size("gy"), lax.axis_size("gz")
    axes = ("grp", "gy", "gz")

    def at(g, y, z):
        return (g * ys + y) * zs + z

    straight = [(at(g, y, z), at(1 - g, y, z)) for g in range(2) for y in range(ys) for z in range(zs) if zs < 2 or y + z > 0]
    parts = [lax.ppermute(row, axes, straight)]
    if zs > 1:
        row = lax.ppermute(row, axes, [(at(g, 0, 0), at(1 - g, 0, 1)) for g in range(2)])
        parts.append(lax.ppermute(row, axes, [(at(g, 0, 1), at(g, 0, 0)) for g in range(2)]))
    return parts


def call(body, name, operands, shapes, flops):
    unique, places = [], []
    for x in operands:
        for i, y in enumerate(unique):
            if x is y:
                places.append(i)
                break
        else:
            places.append(len(unique))
            unique.append(x)

    def kernel(*refs):
        ins = [refs[i] for i in places]
        body(*ins, *refs[len(unique):])

    moved = sum(4 * x.size for x in unique) + sum(4 * functools.reduce(lambda a, b: a * b, s) for s in shapes)
    return pl.pallas_call(
        kernel,
        out_shape=[jax.ShapeDtypeStruct(s, jnp.float32) for s in shapes],
        in_specs=[pl.BlockSpec(memory_space=pltpu.VMEM)] * len(unique),
        out_specs=[pl.BlockSpec(memory_space=pltpu.VMEM)] * len(shapes),
        compiler_params=pltpu.CompilerParams(vmem_limit_bytes=40 * 1024 * 1024),
        cost_estimate=pl.CostEstimate(flops=flops, bytes_accessed=moved, transcendentals=0),
        name=name,
    )(*unique)


def rows(first, stop, step):
    whole = first + (stop - first) // 4 * 4
    lax.fori_loop(first, whole, lambda b, _: step(b), None, unroll=4)
    for b in range(whole, stop):
        step(b)


def iotas(c, d):
    return lax.broadcasted_iota(jnp.int32, (c, d), 0), lax.broadcasted_iota(jnp.int32, (c, d), 1)


def next_c(x, halo, row):
    c = x.shape[0]
    return jnp.where(row == c - 1, halo, pltpu.roll(x, c - 1, 0))


def prev_c(x, halo, row):
    return jnp.where(row == 0, halo, pltpu.roll(x, 1, 0))


def next_d(x, other, lane):
    d = x.shape[1]
    return pltpu.roll(jnp.where(lane == 0, other, x), d - 1, 1)


def prev_d(x, other, lane):
    d = x.shape[1]
    return pltpu.roll(jnp.where(lane == d - 1, other, x), 1, 1)


def prev_b(ref, halo, b):
    return jnp.where(b == 0, halo, ref[0, jnp.maximum(b - 1, 0)])


def next_b(ref, halo, b, count):
    return jnp.where(b == count - 1, halo, ref[0, jnp.minimum(b + 1, count - 1)])


def pack_d(field, low, high, lane):
    d = field.shape[1]
    return jnp.where((lane == 0) | (lane == d - 1), field, pltpu.roll(jnp.where(lane == 0, low, high), d // 2, 1))


def unpack_d(packed):
    return pltpu.roll(packed, packed.shape[1] // 2, 1)


def neighbours(ref, before_b, after_b, gz_before, gz_after, wa_before, wa_after, b, row, lane):
    count = ref.shape[1]
    x = ref[0, b]
    return [
        next_b(ref, after_b[0], b, count),
        prev_b(ref, before_b[0], b),
        next_c(x, gz_after[1, pl.ds(b, 1), :], row),
        prev_c(x, gz_before[0, pl.ds(b, 1), :], row),
        next_d(x, wa_after[0, b], lane),
        prev_d(x, wa_before[0, b], lane),
    ]


def prepare_body(pair, rates, labels, cot, start, f_ref, g_ref, w_ref, up_ref, down_ref, gz_ref, *u_refs):
    count, c, d = g_ref.shape[1:]
    row, lane = iotas(c, d)

    def step(b, u, shift):
        r = [rates[j, 0, b] for j in range(8)]
        total = ((r[0] + r[1]) + (r[2] + r[3])) + ((r[4] + r[5]) + (r[6] + r[7]))
        f = jnp.where(labels[0, b] == 0, DAMP / total, 0.0)
        g = f * cot[0, b]
        f_ref[0, b] = f
        g_ref[0, b] = g
        if pair:
            u[0, b - shift] = (r[0] + r[1]) * g
        else:
            u_refs[0][0, b] = r[0] * g
            u_refs[1][0, b] = r[1] * g
        w_ref[0, b] = pack_d(start[0, b], r[7] * g, r[6] * g, lane)
        gz_ref[0, pl.ds(b, 1), :] = start[0, b, c - 1 :, :]
        gz_ref[1, pl.ds(b, 1), :] = start[0, b, :1, :]
        gz_ref[2, pl.ds(b, 1), :] = (r[4] * g)[c - 1 :]
        gz_ref[3, pl.ds(b, 1), :] = (r[5] * g)[:1]

    if pair:
        rows(0, count - 1, lambda b: step(b, u_refs[0], 0))
        step(count - 1, u_refs[1], count - 1)
    else:
        rows(0, count, lambda b: step(b, None, 0))
    up_ref[0] = start[0, count - 1]
    up_ref[1] = rates[2, 0, count - 1] * g_ref[0, count - 1]
    down_ref[0] = start[0, 0]
    down_ref[1] = rates[3, 0, 0] * g_ref[0, 0]


def forward_body(pair, rates, f_ref, labels, q, q_before, q_after, up, down, gz_before, gz_after, wa_before, wa_after, first, s_ref):
    count, c, d = q.shape[1:]
    row, lane = iotas(c, d)

    def step(b):
        f = f_ref[0, b]
        near = neighbours(q, up, down, gz_before, gz_after, wa_before, wa_after, b, row, lane)
        total = sum(rates[2 + k, 0, b] * near[k] for k in range(6))
        if pair:
            total = total + (rates[0, 0, b] + rates[1, 0, b]) * q_after[0, b]
        else:
            total = total + rates[0, 0, b] * q_after[0, b] + rates[1, 0, b] * q_before[0, b]
        s = f * total
        label = labels[0, b]
        s_ref[0, b] = s
        first[0, b] = jnp.where(label == 0, KEEP * q[0, b] + s, jnp.where(label == 2, 1.0, 0.0))

    rows(0, count, step)


def spread(rates, f_ref, x, g, up, down, gz_before, gz_after, wa_before, wa_after, at, b, row, lane):
    count, c, d = g.shape[1:]
    f, own = f_ref[0, b], g[0, b]
    below, above = jnp.maximum(b - 1, 0), jnp.minimum(b + 1, count - 1)
    out = jnp.where(f > 0.0, KEEP * x, 0.0)
    out = out + jnp.where(b == 0, up[at], rates[2, 0, below] * g[0, below])
    out = out + jnp.where(b == count - 1, down[at], rates[3, 0, above] * g[0, above])
    out = out + prev_c(rates[4, 0, b] * own, gz_before[2 * at, pl.ds(b, 1), :], row)
    out = out + next_c(rates[5, 0, b] * own, gz_after[2 * at + 1, pl.ds(b, 1), :], row)
    out = out + prev_d(rates[6, 0, b] * own, unpack_d(wa_before[0, b]), lane)
    out = out + next_d(rates[7, 0, b] * own, unpack_d(wa_after[0, b]), lane)
    return out


def back_body(pair, parts, rates, f_ref, cot, g, u_before, u_after, *refs):
    u_row, refs = refs[:parts], refs[parts:]
    back_rows(pair, rates, f_ref, cot, g, u_before, u_after, u_row, *refs)


def back_rows(pair, rates, f_ref, cot, g, u_before, u_after, u_row, up, down, gz_before, gz_after, wa_before, wa_after, first,
              back, h_ref, w_ref, up_ref, down_ref, gz_ref, *v_refs):
    count, c, d = g.shape[1:]
    row, lane = iotas(c, d)

    half = len(v_refs) // 2
    cut = v_refs[0].shape[1]

    def step(b, v, shift, came=None):
        out = spread(rates, f_ref, cot[0, b], g, up, down, gz_before, gz_after, wa_before, wa_after, 1, b, row, lane)
        if came:
            for ref in came:
                out = out + ref[0, 0]
        elif pair:
            out = out + u_before[0, b]
        else:
            out = out + u_before[0, b] + u_after[0, b]
        h = f_ref[0, b] * out
        back[0, b] = out
        h_ref[0, b] = h
        if pair:
            v[0][0, b - shift] = (rates[0, 0, b] + rates[1, 0, b]) * h
        else:
            v[0][0, b - shift] = rates[0, 0, b] * h
            v[1][0, b - shift] = rates[1, 0, b] * h
        w_ref[0, b] = pack_d(first[0, b], rates[7, 0, b] * h, rates[6, 0, b] * h, lane)
        gz_ref[0, pl.ds(b, 1), :] = first[0, b, c - 1 :, :]
        gz_ref[1, pl.ds(b, 1), :] = first[0, b, :1, :]
        gz_ref[2, pl.ds(b, 1), :] = (rates[4, 0, b] * h)[c - 1 :]
        gz_ref[3, pl.ds(b, 1), :] = (rates[5, 0, b] * h)[:1]

    rows(0, cut, lambda b: step(b, v_refs[:half], 0))
    stop = count - 1 if pair else count
    rows(cut, stop, lambda b: step(b, v_refs[half:], cut))
    if pair:
        step(stop, v_refs[half:], cut, u_row)
    up_ref[0] = first[0, count - 1]
    up_ref[1] = rates[2, 0, count - 1] * h_ref[0, count - 1]
    down_ref[0] = first[0, 0]
    down_ref[1] = rates[3, 0, 0] * h_ref[0, 0]


def last_body(rates, f_ref, labels, g, h, s_ref, start, start_before, start_after, up0, down0, gz_before0, gz_after0, wa_before0,
              wa_after0, first, first_before, first_after, up1, down1, gz_before1, gz_after1, wa_before1, wa_after1, back, committor, out, partial):
    count, c, d = first.shape[1:]
    row, lane = iotas(c, d)

    def step(b):
        f = f_ref[0, b]
        near1 = [first_after[0, b], first_before[0, b]]
        near1 += neighbours(first, up1, down1, gz_before1, gz_after1, wa_before1, wa_after1, b, row, lane)
        s1 = f * sum(rates[k, 0, b] * near1[k] for k in range(8))
        label = labels[0, b]
        committor[0, b] = jnp.where(label == 0, KEEP * first[0, b] + s1, jnp.where(label == 2, 1.0, 0.0))
        near0 = [start_after[0, b], start_before[0, b]]
        near0 += neighbours(start, up0, down0, gz_before0, gz_after0, wa_before0, wa_after0, b, row, lane)
        avg1, avg0 = s1 * (1.0 / DAMP), s_ref[0, b] * (1.0 / DAMP)
        gb, hb = g[0, b], h[0, b]
        for k in range(8):
            out[k, 0, b] = gb * (near1[k] - avg1) + hb * (near0[k] - avg0)
        partial[0, b] = spread(rates, f_ref, back[0, b], h, up1, down1, gz_before1, gz_after1, wa_before1, wa_after1, 1, b, row, lane)

    rows(0, count, step)


def finish(grad, came):
    parts = [came[0]] if came[0] is came[1] else list(came)
    shape = came[0].shape

    def kernel(*refs):
        grad_ref, came_refs, (out, total, sem) = refs[0], refs[1:-3], refs[-3:]
        acc = grad_ref[0, : shape[1]]
        for ref in came_refs:
            acc = acc + ref[0]
        total[...] = acc
        copy = pltpu.make_async_copy(total, out.at[0, pl.ds(0, shape[1])], sem)
        copy.start()
        copy.wait()

    return pl.pallas_call(
        kernel,
        out_shape=jax.ShapeDtypeStruct(grad.shape, jnp.float32),
        in_specs=[pl.BlockSpec(memory_space=pltpu.VMEM)] * (1 + len(parts)),
        out_specs=pl.BlockSpec(memory_space=pl.ANY),
        scratch_shapes=[pltpu.VMEM(shape[1:], jnp.float32), pltpu.SemaphoreType.DMA],
        compiler_params=pltpu.CompilerParams(vmem_limit_bytes=4 * 1024 * 1024),
        name="finish",
    )(grad, *parts)


def on_device(start, rates, labels, cotangent):
    _, b, c, d = start.shape
    block = (1, b, c, d)
    cells = b * c * d
    pair = lax.axis_size("grp") == 2
    blocks = [block] * (1 if pair else 2)
    tail = max(1, b // 6)
    faces = [(2, c, d), (2, c, d), (4, b, d)]

    start_before, start_after = both_ways(start, start, "grp")
    f, g, w0, up, down, gz, *u = call(
        functools.partial(prepare_body, pair), "prepare", [rates, labels, cotangent, start], [block] * 3 + faces + ([(1, b - 1, c, d), (1, 1, c, d)] if pair else blocks), 20 * cells
    )
    u_before, u_after = both_ways(u[0], u[0] if pair else u[1], "grp")
    u_row = row_swap(u[1]) if pair else []
    up0, down0 = both_ways(up, down, "gy")
    gz_before0, gz_after0 = both_ways(gz, gz, "gz")
    wa0 = both_ways(w0, w0, "wa")

    first, s0 = call(
        functools.partial(forward_body, pair),
        "forward",
        [rates, f, labels, start, start_before, start_after, up0, down0, gz_before0, gz_after0, *wa0],
        [block] * 2,
        30 * cells,
    )
    first_before, first_after = both_ways(first, first, "grp")

    back, h, w1, up, down, gz, *v = call(
        functools.partial(back_body, pair, len(u_row)),
        "backward",
        [rates, f, cotangent, g, u_before, u_after, *u_row, up0, down0, gz_before0, gz_after0, *wa0, first],
        [block] * 3 + faces + [(1, b - tail, c, d)] * len(blocks) + [(1, tail, c, d)] * len(blocks),
        30 * cells,
    )
    most = both_ways(v[0], v[len(blocks) - 1], "grp")
    rest = both_ways(v[len(blocks)], v[-1], "grp")
    up1, down1 = both_ways(up, down, "gy")
    gz_before1, gz_after1 = both_ways(gz, gz, "gz")
    wa1 = both_ways(w1, w1, "wa")

    committor, grad_rates, grad = call(
        last_body,
        "last",
        [rates, f, labels, g, h, s0, start, start_before, start_after, up0, down0, gz_before0, gz_after0, *wa0,
         first, first_before, first_after, up1, down1, gz_before1, gz_after1, *wa1, back],
        [block, (8, 1, b, c, d), block],
        120 * cells,
    )
    last_rows = grad[:, b - tail :] + rest[0]
    if not pair:
        last_rows = last_rows + rest[1]
    grad_start = lax.dynamic_update_slice(finish(grad, most), last_rows, (0, b - tail, 0, 0))
    return committor, grad_start, grad_rates


def solution(mesh):
    placed = (
        P("grp", "gy", "gz", "wa"),
        P(None, "grp", "gy", "gz", "wa"),
        P("grp", "gy", "gz", "wa"),
        P("grp", "gy", "gz", "wa"),
    )
    return jax.shard_map(
        on_device,
        mesh=mesh,
        in_specs=placed,
        out_specs=(
            P("grp", "gy", "gz", "wa"),
            P("grp", "gy", "gz", "wa"),
            P(None, "grp", "gy", "gz", "wa"),
        ),
        check_vma=False,
    )
```

```python
import functools

import jax
import jax.numpy as jnp
from jax import lax
from jax.experimental import pallas as pl
from jax.experimental.pallas import tpu as pltpu
from jax.sharding import PartitionSpec as P

DAMP = 0.8
KEEP = 1.0 - 0.8


def ring(axis, distance):
    size = lax.axis_size(axis)
    return [(i, (i + distance) % size) for i in range(size)]


def both_ways(up, down, axis):
    if lax.axis_size(axis) == 2 and up is down:
        other = lax.ppermute(up, axis, ring(axis, 1))
        return other, other
    return lax.ppermute(up, axis, ring(axis, 1)), lax.ppermute(down, axis, ring(axis, -1))


def part_swap(part):
    ys, zs, ws = lax.axis_size("gy"), lax.axis_size("gz"), lax.axis_size("wa")
    axes = ("grp", "gy", "gz", "wa")

    def at(g, y, z, w):
        return ((g * ys + y) * zs + z) * ws + w

    def middle(g, w):
        return at(1 - g, 0, 1, w) if w == 0 or ys == 1 else at(1 - g, 1, 0, w)

    cells = [(g, y, z, w) for g in range(2) for y in range(ys) for z in range(zs) for w in range(ws)]
    straight = [(at(g, y, z, w), at(1 - g, y, z, w)) for g, y, z, w in cells if zs < 2 or y + z > 0]
    parts = [lax.ppermute(part, axes, straight)]
    if zs > 1:
        ends = [(g, w) for g in range(2) for w in range(ws)]
        part = lax.ppermute(part, axes, [(at(g, 0, 0, w), middle(g, w)) for g, w in ends])
        parts.append(lax.ppermute(part, axes, [(middle(g, w), at(1 - g, 0, 0, w)) for g, w in ends]))
    return parts


def part_lines(c):
    return c + c // 3 // 8 * 8


def call(body, name, operands, shapes, flops):
    unique, places = [], []
    for x in operands:
        for i, y in enumerate(unique):
            if x is y:
                places.append(i)
                break
        else:
            places.append(len(unique))
            unique.append(x)

    def kernel(*refs):
        ins = [refs[i] for i in places]
        body(*ins, *refs[len(unique):])

    moved = sum(4 * x.size for x in unique) + sum(4 * functools.reduce(lambda a, b: a * b, s) for s in shapes)
    return pl.pallas_call(
        kernel,
        out_shape=[jax.ShapeDtypeStruct(s, jnp.float32) for s in shapes],
        in_specs=[pl.BlockSpec(memory_space=pltpu.VMEM)] * len(unique),
        out_specs=[pl.BlockSpec(memory_space=pltpu.VMEM)] * len(shapes),
        compiler_params=pltpu.CompilerParams(vmem_limit_bytes=40 * 1024 * 1024),
        cost_estimate=pl.CostEstimate(flops=flops, bytes_accessed=moved, transcendentals=0),
        name=name,
    )(*unique)


def rows(first, stop, step):
    whole = first + (stop - first) // 4 * 4
    lax.fori_loop(first, whole, lambda b, _: step(b), None, unroll=4)
    for b in range(whole, stop):
        step(b)


def iotas(c, d):
    return lax.broadcasted_iota(jnp.int32, (c, d), 0), lax.broadcasted_iota(jnp.int32, (c, d), 1)


def next_c(x, halo, row):
    c = x.shape[0]
    return jnp.where(row == c - 1, halo, pltpu.roll(x, c - 1, 0))


def prev_c(x, halo, row):
    return jnp.where(row == 0, halo, pltpu.roll(x, 1, 0))


def next_d(x, other, lane):
    d = x.shape[1]
    return pltpu.roll(jnp.where(lane == 0, other, x), d - 1, 1)


def prev_d(x, other, lane):
    d = x.shape[1]
    return pltpu.roll(jnp.where(lane == d - 1, other, x), 1, 1)


def prev_b(ref, halo, b):
    return jnp.where(b == 0, halo, ref[0, jnp.maximum(b - 1, 0)])


def next_b(ref, halo, b, count):
    return jnp.where(b == count - 1, halo, ref[0, jnp.minimum(b + 1, count - 1)])


def pack_d(field, low, high, lane):
    d = field.shape[1]
    return jnp.where((lane == 0) | (lane == d - 1), field, pltpu.roll(jnp.where(lane == 0, low, high), d // 2, 1))


def unpack_d(packed):
    return pltpu.roll(packed, packed.shape[1] // 2, 1)


def neighbours(ref, before_b, after_b, gz_before, gz_after, wa_before, wa_after, b, row, lane):
    count = ref.shape[1]
    x = ref[0, b]
    return [
        next_b(ref, after_b[0], b, count),
        prev_b(ref, before_b[0], b),
        next_c(x, gz_after[1, pl.ds(b, 1), :], row),
        prev_c(x, gz_before[0, pl.ds(b, 1), :], row),
        next_d(x, wa_after[0, b], lane),
        prev_d(x, wa_before[0, b], lane),
    ]


def prepare_body(pair, rates, labels, cot, start, f_ref, g_ref, w_ref, up_ref, down_ref, gz_ref, *u_refs):
    count, c, d = g_ref.shape[1:]
    row, lane = iotas(c, d)

    def step(b, places):
        r = [rates[j, 0, b] for j in range(8)]
        total = ((r[0] + r[1]) + (r[2] + r[3])) + ((r[4] + r[5]) + (r[6] + r[7]))
        f = jnp.where(labels[0, b] == 0, DAMP / total, 0.0)
        g = f * cot[0, b]
        f_ref[0, b] = f
        g_ref[0, b] = g
        if pair:
            for ref, to, lines in places:
                ref[0, to, :] = ((r[0] + r[1]) * g)[lines]
        else:
            u_refs[0][0, b] = r[0] * g
            u_refs[1][0, b] = r[1] * g
        w_ref[0, b] = pack_d(start[0, b], r[7] * g, r[6] * g, lane)
        gz_ref[0, pl.ds(b, 1), :] = start[0, b, c - 1 :, :]
        gz_ref[1, pl.ds(b, 1), :] = start[0, b, :1, :]
        gz_ref[2, pl.ds(b, 1), :] = (r[4] * g)[c - 1 :]
        gz_ref[3, pl.ds(b, 1), :] = (r[5] * g)[:1]

    if pair:
        most, part = u_refs
        over = part.shape[1] - c
        rows(0, count - 2, lambda b: step(b, [(most, pl.ds(pl.multiple_of(b * c, 8), c), slice(None))]))
        mixed = [(most, pl.ds((count - 2) * c, c - over), slice(0, c - over))]
        step(count - 2, mixed + ([(part, pl.ds(0, over), slice(c - over, c))] if over else []))
        step(count - 1, [(part, pl.ds(over, c), slice(None))])
    else:
        rows(0, count, lambda b: step(b, []))
    up_ref[0] = start[0, count - 1]
    up_ref[1] = rates[2, 0, count - 1] * g_ref[0, count - 1]
    down_ref[0] = start[0, 0]
    down_ref[1] = rates[3, 0, 0] * g_ref[0, 0]


def forward_body(pair, rates, f_ref, labels, q, q_before, q_after, up, down, gz_before, gz_after, wa_before, wa_after, first, s_ref):
    count, c, d = q.shape[1:]
    row, lane = iotas(c, d)

    def step(b):
        f = f_ref[0, b]
        near = neighbours(q, up, down, gz_before, gz_after, wa_before, wa_after, b, row, lane)
        total = sum(rates[2 + k, 0, b] * near[k] for k in range(6))
        if pair:
            total = total + (rates[0, 0, b] + rates[1, 0, b]) * q_after[0, b]
        else:
            total = total + rates[0, 0, b] * q_after[0, b] + rates[1, 0, b] * q_before[0, b]
        s = f * total
        label = labels[0, b]
        s_ref[0, b] = s
        first[0, b] = jnp.where(label == 0, KEEP * q[0, b] + s, jnp.where(label == 2, 1.0, 0.0))

    rows(0, count, step)


def spread(rates, f_ref, x, g, up, down, gz_before, gz_after, wa_before, wa_after, at, b, row, lane):
    count, c, d = g.shape[1:]
    f, own = f_ref[0, b], g[0, b]
    below, above = jnp.maximum(b - 1, 0), jnp.minimum(b + 1, count - 1)
    out = jnp.where(f > 0.0, KEEP * x, 0.0)
    out = out + jnp.where(b == 0, up[at], rates[2, 0, below] * g[0, below])
    out = out + jnp.where(b == count - 1, down[at], rates[3, 0, above] * g[0, above])
    out = out + prev_c(rates[4, 0, b] * own, gz_before[2 * at, pl.ds(b, 1), :], row)
    out = out + next_c(rates[5, 0, b] * own, gz_after[2 * at + 1, pl.ds(b, 1), :], row)
    out = out + prev_d(rates[6, 0, b] * own, unpack_d(wa_before[0, b]), lane)
    out = out + next_d(rates[7, 0, b] * own, unpack_d(wa_after[0, b]), lane)
    return out


def back_body(pair, parts, rates, f_ref, cot, g, u_before, u_after, *refs):
    u_row, refs = refs[:parts], refs[parts:]
    back_rows(pair, rates, f_ref, cot, g, u_before, u_after, u_row, *refs)


def back_rows(pair, rates, f_ref, cot, g, u_before, u_after, u_row, up, down, gz_before, gz_after, wa_before, wa_after, first,
              back, h_ref, w_ref, up_ref, down_ref, gz_ref, *v_refs):
    count, c, d = g.shape[1:]
    row, lane = iotas(c, d)

    half = len(v_refs) // 2
    cut = v_refs[0].shape[1]

    def step(b, v, shift, came=None):
        out = spread(rates, f_ref, cot[0, b], g, up, down, gz_before, gz_after, wa_before, wa_after, 1, b, row, lane)
        if came:
            out = out + came(b)
        else:
            out = out + u_before[0, b] + u_after[0, b]
        h = f_ref[0, b] * out
        back[0, b] = out
        h_ref[0, b] = h
        if pair:
            v[0][0, b - shift] = (rates[0, 0, b] + rates[1, 0, b]) * h
        else:
            v[0][0, b - shift] = rates[0, 0, b] * h
            v[1][0, b - shift] = rates[1, 0, b] * h
        w_ref[0, b] = pack_d(first[0, b], rates[7, 0, b] * h, rates[6, 0, b] * h, lane)
        gz_ref[0, pl.ds(b, 1), :] = first[0, b, c - 1 :, :]
        gz_ref[1, pl.ds(b, 1), :] = first[0, b, :1, :]
        gz_ref[2, pl.ds(b, 1), :] = (rates[4, 0, b] * h)[c - 1 :]
        gz_ref[3, pl.ds(b, 1), :] = (rates[5, 0, b] * h)[:1]

    if not pair:
        rows(0, cut, lambda b: step(b, v_refs[:half], 0))
        rows(cut, count, lambda b: step(b, v_refs[half:], cut))
    else:
        over = u_row[0].shape[1] - c

        def part(first, lines):
            return sum(ref[0, first : first + lines] for ref in u_row)

        def most(b):
            return u_before[0, pl.ds(pl.multiple_of(b * c, 8), c), :]

        def mixed(b):
            return jnp.concatenate([u_before[0, pl.ds(b * c, c - over), :], part(0, over)], axis=0)

        rows(0, cut, lambda b: step(b, v_refs[:half], 0, most))
        rows(cut, count - 2, lambda b: step(b, v_refs[half:], cut, most))
        step(count - 2, v_refs[half:], cut, mixed if over else most)
        step(count - 1, v_refs[half:], cut, lambda b: part(over, c))
    up_ref[0] = first[0, count - 1]
    up_ref[1] = rates[2, 0, count - 1] * h_ref[0, count - 1]
    down_ref[0] = first[0, 0]
    down_ref[1] = rates[3, 0, 0] * h_ref[0, 0]


def last_body(rates, f_ref, labels, g, h, s_ref, start, start_before, start_after, up0, down0, gz_before0, gz_after0, wa_before0,
              wa_after0, first, first_before, first_after, up1, down1, gz_before1, gz_after1, wa_before1, wa_after1, back, committor, out, partial):
    count, c, d = first.shape[1:]
    row, lane = iotas(c, d)

    def step(b):
        f = f_ref[0, b]
        near1 = [first_after[0, b], first_before[0, b]]
        near1 += neighbours(first, up1, down1, gz_before1, gz_after1, wa_before1, wa_after1, b, row, lane)
        s1 = f * sum(rates[k, 0, b] * near1[k] for k in range(8))
        label = labels[0, b]
        committor[0, b] = jnp.where(label == 0, KEEP * first[0, b] + s1, jnp.where(label == 2, 1.0, 0.0))
        near0 = [start_after[0, b], start_before[0, b]]
        near0 += neighbours(start, up0, down0, gz_before0, gz_after0, wa_before0, wa_after0, b, row, lane)
        avg1, avg0 = s1 * (1.0 / DAMP), s_ref[0, b] * (1.0 / DAMP)
        gb, hb = g[0, b], h[0, b]
        for k in range(8):
            out[k, 0, b] = gb * (near1[k] - avg1) + hb * (near0[k] - avg0)
        partial[0, b] = spread(rates, f_ref, back[0, b], h, up1, down1, gz_before1, gz_after1, wa_before1, wa_after1, 1, b, row, lane)

    rows(0, count, step)


def finish(grad, came):
    parts = [came[0]] if came[0] is came[1] else list(came)
    shape = came[0].shape

    def kernel(*refs):
        grad_ref, came_refs, (out, total, sem) = refs[0], refs[1:-3], refs[-3:]
        acc = grad_ref[0, : shape[1]]
        for ref in came_refs:
            acc = acc + ref[0]
        total[...] = acc
        copy = pltpu.make_async_copy(total, out.at[0, pl.ds(0, shape[1])], sem)
        copy.start()
        copy.wait()

    return pl.pallas_call(
        kernel,
        out_shape=jax.ShapeDtypeStruct(grad.shape, jnp.float32),
        in_specs=[pl.BlockSpec(memory_space=pltpu.VMEM)] * (1 + len(parts)),
        out_specs=pl.BlockSpec(memory_space=pl.ANY),
        scratch_shapes=[pltpu.VMEM(shape[1:], jnp.float32), pltpu.SemaphoreType.DMA],
        compiler_params=pltpu.CompilerParams(vmem_limit_bytes=4 * 1024 * 1024),
        name="finish",
    )(grad, *parts)


def on_device(start, rates, labels, cotangent):
    _, b, c, d = start.shape
    block = (1, b, c, d)
    cells = b * c * d
    pair = lax.axis_size("grp") == 2
    blocks = [block] * (1 if pair else 2)
    tail = max(1, b // 6)
    faces = [(2, c, d), (2, c, d), (4, b, d)]

    start_before, start_after = both_ways(start, start, "grp")
    f, g, w0, up, down, gz, *u = call(
        functools.partial(prepare_body, pair), "prepare", [rates, labels, cotangent, start], [block] * 3 + faces + ([(1, b * c - part_lines(c), d), (1, part_lines(c), d)] if pair else blocks), 20 * cells
    )
    u_before, u_after = both_ways(u[0], u[0] if pair else u[1], "grp")
    u_row = part_swap(u[1]) if pair else []
    up0, down0 = both_ways(up, down, "gy")
    gz_before0, gz_after0 = both_ways(gz, gz, "gz")
    wa0 = both_ways(w0, w0, "wa")

    first, s0 = call(
        functools.partial(forward_body, pair),
        "forward",
        [rates, f, labels, start, start_before, start_after, up0, down0, gz_before0, gz_after0, *wa0],
        [block] * 2,
        30 * cells,
    )
    first_before, first_after = both_ways(first, first, "grp")

    back, h, w1, up, down, gz, *v = call(
        functools.partial(back_body, pair, len(u_row)),
        "backward",
        [rates, f, cotangent, g, u_before, u_after, *u_row, up0, down0, gz_before0, gz_after0, *wa0, first],
        [block] * 3 + faces + [(1, b - tail, c, d)] * len(blocks) + [(1, tail, c, d)] * len(blocks),
        30 * cells,
    )
    most = both_ways(v[0], v[len(blocks) - 1], "grp")
    rest = both_ways(v[len(blocks)], v[-1], "grp")
    up1, down1 = both_ways(up, down, "gy")
    gz_before1, gz_after1 = both_ways(gz, gz, "gz")
    wa1 = both_ways(w1, w1, "wa")

    committor, grad_rates, grad = call(
        last_body,
        "last",
        [rates, f, labels, g, h, s0, start, start_before, start_after, up0, down0, gz_before0, gz_after0, *wa0,
         first, first_before, first_after, up1, down1, gz_before1, gz_after1, *wa1, back],
        [block, (8, 1, b, c, d), block],
        120 * cells,
    )
    last_rows = grad[:, b - tail :] + rest[0]
    if not pair:
        last_rows = last_rows + rest[1]
    grad_start = lax.dynamic_update_slice(finish(grad, most), last_rows, (0, b - tail, 0, 0))
    return committor, grad_start, grad_rates


def solution(mesh):
    placed = (
        P("grp", "gy", "gz", "wa"),
        P(None, "grp", "gy", "gz", "wa"),
        P("grp", "gy", "gz", "wa"),
        P("grp", "gy", "gz", "wa"),
    )
    return jax.shard_map(
        on_device,
        mesh=mesh,
        in_specs=placed,
        out_specs=(
            P("grp", "gy", "gz", "wa"),
            P("grp", "gy", "gz", "wa"),
            P(None, "grp", "gy", "gz", "wa"),
        ),
        check_vma=False,
    )
```

```python
import functools

import jax
import jax.numpy as jnp
from jax import lax
from jax.experimental import pallas as pl
from jax.experimental.pallas import tpu as pltpu
from jax.sharding import PartitionSpec as P

DAMP = 0.8
KEEP = 1.0 - 0.8


def ring(axis, distance):
    size = lax.axis_size(axis)
    return [(i, (i + distance) % size) for i in range(size)]


def both_ways(up, down, axis):
    if lax.axis_size(axis) == 2 and up is down:
        other = lax.ppermute(up, axis, ring(axis, 1))
        return other, other
    return lax.ppermute(up, axis, ring(axis, 1)), lax.ppermute(down, axis, ring(axis, -1))


def part_swap(part):
    ys, zs, ws = lax.axis_size("gy"), lax.axis_size("gz"), lax.axis_size("wa")
    axes = ("grp", "gy", "gz", "wa")

    def at(g, y, z, w):
        return ((g * ys + y) * zs + z) * ws + w

    def middle(g, w):
        return at(1 - g, 0, 1, w) if w == 0 or ys == 1 else at(1 - g, 1, 0, w)

    cells = [(g, y, z, w) for g in range(2) for y in range(ys) for z in range(zs) for w in range(ws)]
    straight = [(at(g, y, z, w), at(1 - g, y, z, w)) for g, y, z, w in cells if zs < 2 or y + z > 0]
    parts = [lax.ppermute(part, axes, straight)]
    if zs > 1:
        ends = [(g, w) for g in range(2) for w in range(ws)]
        part = lax.ppermute(part, axes, [(at(g, 0, 0, w), middle(g, w)) for g, w in ends])
        parts.append(lax.ppermute(part, axes, [(middle(g, w), at(1 - g, 0, 0, w)) for g, w in ends]))
    return parts


def part_lines(c):
    return c + c // 2 // 8 * 8


def call(body, name, operands, shapes, flops):
    unique, places = [], []
    for x in operands:
        for i, y in enumerate(unique):
            if x is y:
                places.append(i)
                break
        else:
            places.append(len(unique))
            unique.append(x)

    def kernel(*refs):
        ins = [refs[i] for i in places]
        body(*ins, *refs[len(unique):])

    moved = sum(4 * x.size for x in unique) + sum(4 * functools.reduce(lambda a, b: a * b, s) for s in shapes)
    return pl.pallas_call(
        kernel,
        out_shape=[jax.ShapeDtypeStruct(s, jnp.float32) for s in shapes],
        in_specs=[pl.BlockSpec(memory_space=pltpu.VMEM)] * len(unique),
        out_specs=[pl.BlockSpec(memory_space=pltpu.VMEM)] * len(shapes),
        compiler_params=pltpu.CompilerParams(vmem_limit_bytes=40 * 1024 * 1024),
        cost_estimate=pl.CostEstimate(flops=flops, bytes_accessed=moved, transcendentals=0),
        name=name,
    )(*unique)


def rows(first, stop, step):
    whole = first + (stop - first) // 4 * 4
    lax.fori_loop(first, whole, lambda b, _: step(b), None, unroll=4)
    for b in range(whole, stop):
        step(b)


def iotas(c, d):
    return lax.broadcasted_iota(jnp.int32, (c, d), 0), lax.broadcasted_iota(jnp.int32, (c, d), 1)


def next_c(x, halo, row):
    c = x.shape[0]
    return jnp.where(row == c - 1, halo, pltpu.roll(x, c - 1, 0))


def prev_c(x, halo, row):
    return jnp.where(row == 0, halo, pltpu.roll(x, 1, 0))


def next_d(x, other, lane):
    d = x.shape[1]
    return pltpu.roll(jnp.where(lane == 0, other, x), d - 1, 1)


def prev_d(x, other, lane):
    d = x.shape[1]
    return pltpu.roll(jnp.where(lane == d - 1, other, x), 1, 1)


def prev_b(ref, halo, b):
    return jnp.where(b == 0, halo, ref[0, jnp.maximum(b - 1, 0)])


def next_b(ref, halo, b, count):
    return jnp.where(b == count - 1, halo, ref[0, jnp.minimum(b + 1, count - 1)])


def pack_d(field, low, high, lane):
    d = field.shape[1]
    return jnp.where((lane == 0) | (lane == d - 1), field, pltpu.roll(jnp.where(lane == 0, low, high), d // 2, 1))


def unpack_d(packed):
    return pltpu.roll(packed, packed.shape[1] // 2, 1)


def neighbours(ref, before_b, after_b, gz_before, gz_after, wa_before, wa_after, b, row, lane):
    count = ref.shape[1]
    x = ref[0, b]
    return [
        next_b(ref, after_b[0], b, count),
        prev_b(ref, before_b[0], b),
        next_c(x, gz_after[1, pl.ds(b, 1), :], row),
        prev_c(x, gz_before[0, pl.ds(b, 1), :], row),
        next_d(x, wa_after[0, b], lane),
        prev_d(x, wa_before[0, b], lane),
    ]


def prepare_body(pair, rates, labels, cot, start, f_ref, g_ref, w_ref, up_ref, down_ref, gz_ref, *u_refs):
    count, c, d = g_ref.shape[1:]
    row, lane = iotas(c, d)

    def step(b, places):
        r = [rates[j, 0, b] for j in range(8)]
        total = ((r[0] + r[1]) + (r[2] + r[3])) + ((r[4] + r[5]) + (r[6] + r[7]))
        f = jnp.where(labels[0, b] == 0, DAMP / total, 0.0)
        g = f * cot[0, b]
        f_ref[0, b] = f
        g_ref[0, b] = g
        if pair:
            for ref, to, lines in places:
                ref[0, to, :] = ((r[0] + r[1]) * g)[lines]
        else:
            u_refs[0][0, b] = r[0] * g
            u_refs[1][0, b] = r[1] * g
        w_ref[0, b] = pack_d(start[0, b], r[7] * g, r[6] * g, lane)
        gz_ref[0, pl.ds(b, 1), :] = start[0, b, c - 1 :, :]
        gz_ref[1, pl.ds(b, 1), :] = start[0, b, :1, :]
        gz_ref[2, pl.ds(b, 1), :] = (r[4] * g)[c - 1 :]
        gz_ref[3, pl.ds(b, 1), :] = (r[5] * g)[:1]

    if pair:
        most, part = u_refs
        over = part.shape[1] - c
        rows(0, count - 2, lambda b: step(b, [(most, pl.ds(pl.multiple_of(b * c, 8), c), slice(None))]))
        mixed = [(most, pl.ds((count - 2) * c, c - over), slice(0, c - over))]
        step(count - 2, mixed + ([(part, pl.ds(0, over), slice(c - over, c))] if over else []))
        step(count - 1, [(part, pl.ds(over, c), slice(None))])
    else:
        rows(0, count, lambda b: step(b, []))
    up_ref[0] = start[0, count - 1]
    up_ref[1] = rates[2, 0, count - 1] * g_ref[0, count - 1]
    down_ref[0] = start[0, 0]
    down_ref[1] = rates[3, 0, 0] * g_ref[0, 0]


def forward_body(pair, rates, f_ref, labels, q, q_before, q_after, up, down, gz_before, gz_after, wa_before, wa_after, first, s_ref):
    count, c, d = q.shape[1:]
    row, lane = iotas(c, d)

    def step(b):
        f = f_ref[0, b]
        near = neighbours(q, up, down, gz_before, gz_after, wa_before, wa_after, b, row, lane)
        total = sum(rates[2 + k, 0, b] * near[k] for k in range(6))
        if pair:
            total = total + (rates[0, 0, b] + rates[1, 0, b]) * q_after[0, b]
        else:
            total = total + rates[0, 0, b] * q_after[0, b] + rates[1, 0, b] * q_before[0, b]
        s = f * total
        label = labels[0, b]
        s_ref[0, b] = s
        first[0, b] = jnp.where(label == 0, KEEP * q[0, b] + s, jnp.where(label == 2, 1.0, 0.0))

    rows(0, count, step)


def spread(rates, f_ref, x, g, up, down, gz_before, gz_after, wa_before, wa_after, at, b, row, lane):
    count, c, d = g.shape[1:]
    f, own = f_ref[0, b], g[0, b]
    below, above = jnp.maximum(b - 1, 0), jnp.minimum(b + 1, count - 1)
    out = jnp.where(f > 0.0, KEEP * x, 0.0)
    out = out + jnp.where(b == 0, up[at], rates[2, 0, below] * g[0, below])
    out = out + jnp.where(b == count - 1, down[at], rates[3, 0, above] * g[0, above])
    out = out + prev_c(rates[4, 0, b] * own, gz_before[2 * at, pl.ds(b, 1), :], row)
    out = out + next_c(rates[5, 0, b] * own, gz_after[2 * at + 1, pl.ds(b, 1), :], row)
    out = out + prev_d(rates[6, 0, b] * own, unpack_d(wa_before[0, b]), lane)
    out = out + next_d(rates[7, 0, b] * own, unpack_d(wa_after[0, b]), lane)
    return out


def back_body(pair, parts, rates, f_ref, cot, g, u_before, u_after, *refs):
    u_row, refs = refs[:parts], refs[parts:]
    back_rows(pair, rates, f_ref, cot, g, u_before, u_after, u_row, *refs)


def back_rows(pair, rates, f_ref, cot, g, u_before, u_after, u_row, up, down, gz_before, gz_after, wa_before, wa_after, first,
              back, h_ref, w_ref, up_ref, down_ref, gz_ref, *v_refs):
    count, c, d = g.shape[1:]
    row, lane = iotas(c, d)

    half = len(v_refs) // 2
    cut = v_refs[0].shape[1]

    def step(b, v, shift, came=None):
        out = spread(rates, f_ref, cot[0, b], g, up, down, gz_before, gz_after, wa_before, wa_after, 1, b, row, lane)
        if came:
            out = out + came(b)
        else:
            out = out + u_before[0, b] + u_after[0, b]
        h = f_ref[0, b] * out
        back[0, b] = out
        h_ref[0, b] = h
        if pair:
            v[0][0, b - shift] = (rates[0, 0, b] + rates[1, 0, b]) * h
        else:
            v[0][0, b - shift] = rates[0, 0, b] * h
            v[1][0, b - shift] = rates[1, 0, b] * h
        w_ref[0, b] = pack_d(first[0, b], rates[7, 0, b] * h, rates[6, 0, b] * h, lane)
        gz_ref[0, pl.ds(b, 1), :] = first[0, b, c - 1 :, :]
        gz_ref[1, pl.ds(b, 1), :] = first[0, b, :1, :]
        gz_ref[2, pl.ds(b, 1), :] = (rates[4, 0, b] * h)[c - 1 :]
        gz_ref[3, pl.ds(b, 1), :] = (rates[5, 0, b] * h)[:1]

    if not pair:
        rows(0, cut, lambda b: step(b, v_refs[:half], 0))
        rows(cut, count, lambda b: step(b, v_refs[half:], cut))
    else:
        over = u_row[0].shape[1] - c

        def part(first, lines):
            return sum(ref[0, first : first + lines] for ref in u_row)

        def most(b):
            return u_before[0, pl.ds(pl.multiple_of(b * c, 8), c), :]

        def mixed(b):
            return jnp.concatenate([u_before[0, pl.ds(b * c, c - over), :], part(0, over)], axis=0)

        rows(0, cut, lambda b: step(b, v_refs[:half], 0, most))
        rows(cut, count - 2, lambda b: step(b, v_refs[half:], cut, most))
        step(count - 2, v_refs[half:], cut, mixed if over else most)
        step(count - 1, v_refs[half:], cut, lambda b: part(over, c))
    up_ref[0] = first[0, count - 1]
    up_ref[1] = rates[2, 0, count - 1] * h_ref[0, count - 1]
    down_ref[0] = first[0, 0]
    down_ref[1] = rates[3, 0, 0] * h_ref[0, 0]


def last_body(rates, f_ref, labels, g, h, s_ref, start, start_before, start_after, up0, down0, gz_before0, gz_after0, wa_before0,
              wa_after0, first, first_before, first_after, up1, down1, gz_before1, gz_after1, wa_before1, wa_after1, back, committor, out, partial):
    count, c, d = first.shape[1:]
    row, lane = iotas(c, d)

    def step(b):
        f = f_ref[0, b]
        near1 = [first_after[0, b], first_before[0, b]]
        near1 += neighbours(first, up1, down1, gz_before1, gz_after1, wa_before1, wa_after1, b, row, lane)
        s1 = f * sum(rates[k, 0, b] * near1[k] for k in range(8))
        label = labels[0, b]
        committor[0, b] = jnp.where(label == 0, KEEP * first[0, b] + s1, jnp.where(label == 2, 1.0, 0.0))
        near0 = [start_after[0, b], start_before[0, b]]
        near0 += neighbours(start, up0, down0, gz_before0, gz_after0, wa_before0, wa_after0, b, row, lane)
        avg1, avg0 = s1 * (1.0 / DAMP), s_ref[0, b] * (1.0 / DAMP)
        gb, hb = g[0, b], h[0, b]
        for k in range(8):
            out[k, 0, b] = gb * (near1[k] - avg1) + hb * (near0[k] - avg0)
        partial[0, b] = spread(rates, f_ref, back[0, b], h, up1, down1, gz_before1, gz_after1, wa_before1, wa_after1, 1, b, row, lane)

    rows(0, count, step)


def finish(grad, came):
    parts = [came[0]] if came[0] is came[1] else list(came)
    shape = came[0].shape

    def kernel(*refs):
        grad_ref, came_refs, (out, total, sem) = refs[0], refs[1:-3], refs[-3:]
        acc = grad_ref[0, : shape[1]]
        for ref in came_refs:
            acc = acc + ref[0]
        total[...] = acc
        copy = pltpu.make_async_copy(total, out.at[0, pl.ds(0, shape[1])], sem)
        copy.start()
        copy.wait()

    return pl.pallas_call(
        kernel,
        out_shape=jax.ShapeDtypeStruct(grad.shape, jnp.float32),
        in_specs=[pl.BlockSpec(memory_space=pltpu.VMEM)] * (1 + len(parts)),
        out_specs=pl.BlockSpec(memory_space=pl.ANY),
        scratch_shapes=[pltpu.VMEM(shape[1:], jnp.float32), pltpu.SemaphoreType.DMA],
        compiler_params=pltpu.CompilerParams(vmem_limit_bytes=4 * 1024 * 1024),
        name="finish",
    )(grad, *parts)


def on_device(start, rates, labels, cotangent):
    _, b, c, d = start.shape
    block = (1, b, c, d)
    cells = b * c * d
    pair = lax.axis_size("grp") == 2
    blocks = [block] * (1 if pair else 2)
    tail = max(2, b // 6)
    faces = [(2, c, d), (2, c, d), (4, b, d)]

    start_before, start_after = both_ways(start, start, "grp")
    f, g, w0, up, down, gz, *u = call(
        functools.partial(prepare_body, pair), "prepare", [rates, labels, cotangent, start], [block] * 3 + faces + ([(1, b * c - part_lines(c), d), (1, part_lines(c), d)] if pair else blocks), 20 * cells
    )
    u_before, u_after = both_ways(u[0], u[0] if pair else u[1], "grp")
    u_row = part_swap(u[1]) if pair else []
    up0, down0 = both_ways(up, down, "gy")
    gz_before0, gz_after0 = both_ways(gz, gz, "gz")
    wa0 = both_ways(w0, w0, "wa")

    first, s0 = call(
        functools.partial(forward_body, pair),
        "forward",
        [rates, f, labels, start, start_before, start_after, up0, down0, gz_before0, gz_after0, *wa0],
        [block] * 2,
        30 * cells,
    )
    first_before, first_after = both_ways(first, first, "grp")

    back, h, w1, up, down, gz, *v = call(
        functools.partial(back_body, pair, len(u_row)),
        "backward",
        [rates, f, cotangent, g, u_before, u_after, *u_row, up0, down0, gz_before0, gz_after0, *wa0, first],
        [block] * 3 + faces + [(1, b - tail, c, d)] * len(blocks) + [(1, tail, c, d)] * len(blocks),
        30 * cells,
    )
    most = both_ways(v[0], v[len(blocks) - 1], "grp")
    rest = both_ways(v[len(blocks)], v[-1], "grp")
    up1, down1 = both_ways(up, down, "gy")
    gz_before1, gz_after1 = both_ways(gz, gz, "gz")
    wa1 = both_ways(w1, w1, "wa")

    committor, grad_rates, grad = call(
        last_body,
        "last",
        [rates, f, labels, g, h, s0, start, start_before, start_after, up0, down0, gz_before0, gz_after0, *wa0,
         first, first_before, first_after, up1, down1, gz_before1, gz_after1, *wa1, back],
        [block, (8, 1, b, c, d), block],
        120 * cells,
    )
    last_rows = grad[:, b - tail :] + rest[0]
    if not pair:
        last_rows = last_rows + rest[1]
    grad_start = lax.dynamic_update_slice(finish(grad, most), last_rows, (0, b - tail, 0, 0))
    return committor, grad_start, grad_rates


def solution(mesh):
    placed = (
        P("grp", "gy", "gz", "wa"),
        P(None, "grp", "gy", "gz", "wa"),
        P("grp", "gy", "gz", "wa"),
        P("grp", "gy", "gz", "wa"),
    )
    return jax.shard_map(
        on_device,
        mesh=mesh,
        in_specs=placed,
        out_specs=(
            P("grp", "gy", "gz", "wa"),
            P("grp", "gy", "gz", "wa"),
            P(None, "grp", "gy", "gz", "wa"),
        ),
        check_vma=False,
    )
```

```python
import functools

import jax
import jax.numpy as jnp
from jax import lax
from jax.experimental import pallas as pl
from jax.experimental.pallas import tpu as pltpu
from jax.sharding import PartitionSpec as P

DAMP = 0.8
KEEP = 1.0 - 0.8


def ring(axis, distance):
    size = lax.axis_size(axis)
    return [(i, (i + distance) % size) for i in range(size)]


def both_ways(up, down, axis):
    if lax.axis_size(axis) == 2 and up is down:
        other = lax.ppermute(up, axis, ring(axis, 1))
        return other, other
    return lax.ppermute(up, axis, ring(axis, 1)), lax.ppermute(down, axis, ring(axis, -1))


def part_swap(part):
    ys, zs, ws = lax.axis_size("gy"), lax.axis_size("gz"), lax.axis_size("wa")
    axes = ("grp", "gy", "gz", "wa")

    def at(g, y, z, w):
        return ((g * ys + y) * zs + z) * ws + w

    def middle(g, w):
        return at(1 - g, 0, 1, w) if w == 0 or ys == 1 else at(1 - g, 1, 0, w)

    cells = [(g, y, z, w) for g in range(2) for y in range(ys) for z in range(zs) for w in range(ws)]
    straight = [(at(g, y, z, w), at(1 - g, y, z, w)) for g, y, z, w in cells if zs < 2 or y + z > 0]
    parts = [lax.ppermute(part, axes, straight)]
    if zs > 1:
        ends = [(g, w) for g in range(2) for w in range(ws)]
        part = lax.ppermute(part, axes, [(at(g, 0, 0, w), middle(g, w)) for g, w in ends])
        parts.append(lax.ppermute(part, axes, [(middle(g, w), at(1 - g, 0, 0, w)) for g, w in ends]))
    return parts


def part_lines(c):
    return c + c // 3 // 8 * 8


def call(body, name, operands, shapes, flops):
    unique, places = [], []
    for x in operands:
        for i, y in enumerate(unique):
            if x is y:
                places.append(i)
                break
        else:
            places.append(len(unique))
            unique.append(x)

    def kernel(*refs):
        ins = [refs[i] for i in places]
        body(*ins, *refs[len(unique):])

    moved = sum(4 * x.size for x in unique) + sum(4 * functools.reduce(lambda a, b: a * b, s) for s in shapes)
    return pl.pallas_call(
        kernel,
        out_shape=[jax.ShapeDtypeStruct(s, jnp.float32) for s in shapes],
        in_specs=[pl.BlockSpec(memory_space=pltpu.VMEM)] * len(unique),
        out_specs=[pl.BlockSpec(memory_space=pltpu.VMEM)] * len(shapes),
        compiler_params=pltpu.CompilerParams(vmem_limit_bytes=40 * 1024 * 1024),
        cost_estimate=pl.CostEstimate(flops=flops, bytes_accessed=moved, transcendentals=0),
        name=name,
    )(*unique)


def rows(first, stop, step):
    whole = first + (stop - first) // 4 * 4
    lax.fori_loop(first, whole, lambda b, _: step(b), None, unroll=4)
    for b in range(whole, stop):
        step(b)


def iotas(c, d):
    return lax.broadcasted_iota(jnp.int32, (c, d), 0), lax.broadcasted_iota(jnp.int32, (c, d), 1)


def next_c(x, halo, row):
    c = x.shape[0]
    return jnp.where(row == c - 1, halo, pltpu.roll(x, c - 1, 0))


def prev_c(x, halo, row):
    return jnp.where(row == 0, halo, pltpu.roll(x, 1, 0))


def next_d(x, other, lane):
    d = x.shape[1]
    return pltpu.roll(jnp.where(lane == 0, other, x), d - 1, 1)


def prev_d(x, other, lane):
    d = x.shape[1]
    return pltpu.roll(jnp.where(lane == d - 1, other, x), 1, 1)


def prev_b(ref, halo, b):
    return jnp.where(b == 0, halo, ref[0, jnp.maximum(b - 1, 0)])


def next_b(ref, halo, b, count):
    return jnp.where(b == count - 1, halo, ref[0, jnp.minimum(b + 1, count - 1)])


def pack_d(field, low, high, lane):
    d = field.shape[1]
    return jnp.where((lane == 0) | (lane == d - 1), field, pltpu.roll(jnp.where(lane == 0, low, high), d // 2, 1))


def unpack_d(packed):
    return pltpu.roll(packed, packed.shape[1] // 2, 1)


def neighbours(ref, before_b, after_b, gz_before, gz_after, wa_before, wa_after, b, row, lane):
    count = ref.shape[1]
    x = ref[0, b]
    return [
        next_b(ref, after_b[0], b, count),
        prev_b(ref, before_b[0], b),
        next_c(x, gz_after[1, pl.ds(b, 1), :], row),
        prev_c(x, gz_before[0, pl.ds(b, 1), :], row),
        next_d(x, wa_after[0, b], lane),
        prev_d(x, wa_before[0, b], lane),
    ]


def prepare_body(pair, rates, labels, cot, start, f_ref, g_ref, w_ref, up_ref, down_ref, gz_ref, *u_refs):
    count, c, d = g_ref.shape[1:]
    row, lane = iotas(c, d)

    def step(b, places):
        r = [rates[j, 0, b] for j in range(8)]
        total = ((r[0] + r[1]) + (r[2] + r[3])) + ((r[4] + r[5]) + (r[6] + r[7]))
        f = jnp.where(labels[0, b] == 0, DAMP / total, 0.0)
        g = f * cot[0, b]
        f_ref[0, b] = f
        g_ref[0, b] = g
        if pair:
            for ref, to, lines in places:
                ref[0, to, :] = ((r[0] + r[1]) * g)[lines]
        else:
            u_refs[0][0, b] = r[0] * g
            u_refs[1][0, b] = r[1] * g
        w_ref[0, b] = pack_d(start[0, b], r[7] * g, r[6] * g, lane)
        gz_ref[0, pl.ds(b, 1), :] = start[0, b, c - 1 :, :]
        gz_ref[1, pl.ds(b, 1), :] = start[0, b, :1, :]
        gz_ref[2, pl.ds(b, 1), :] = (r[4] * g)[c - 1 :]
        gz_ref[3, pl.ds(b, 1), :] = (r[5] * g)[:1]

    if pair:
        most, part = u_refs
        over = part.shape[1] - c
        rows(0, count - 2, lambda b: step(b, [(most, pl.ds(pl.multiple_of(b * c, 8), c), slice(None))]))
        mixed = [(most, pl.ds((count - 2) * c, c - over), slice(0, c - over))]
        step(count - 2, mixed + ([(part, pl.ds(0, over), slice(c - over, c))] if over else []))
        step(count - 1, [(part, pl.ds(over, c), slice(None))])
    else:
        rows(0, count, lambda b: step(b, []))
    up_ref[0] = start[0, count - 1]
    up_ref[1] = rates[2, 0, count - 1] * g_ref[0, count - 1]
    down_ref[0] = start[0, 0]
    down_ref[1] = rates[3, 0, 0] * g_ref[0, 0]


def forward_body(pair, rates, f_ref, labels, q, q_before, q_after, up, down, gz_before, gz_after, wa_before, wa_after, first, s_ref):
    count, c, d = q.shape[1:]
    row, lane = iotas(c, d)

    def step(b):
        f = f_ref[0, b]
        near = neighbours(q, up, down, gz_before, gz_after, wa_before, wa_after, b, row, lane)
        total = sum(rates[2 + k, 0, b] * near[k] for k in range(6))
        if pair:
            total = total + (rates[0, 0, b] + rates[1, 0, b]) * q_after[0, b]
        else:
            total = total + rates[0, 0, b] * q_after[0, b] + rates[1, 0, b] * q_before[0, b]
        s = f * total
        label = labels[0, b]
        s_ref[0, b] = s
        first[0, b] = jnp.where(label == 0, KEEP * q[0, b] + s, jnp.where(label == 2, 1.0, 0.0))

    rows(0, count, step)


def spread(rates, f_ref, x, g, up, down, gz_before, gz_after, wa_before, wa_after, at, b, row, lane):
    count, c, d = g.shape[1:]
    f, own = f_ref[0, b], g[0, b]
    below, above = jnp.maximum(b - 1, 0), jnp.minimum(b + 1, count - 1)
    out = jnp.where(f > 0.0, KEEP * x, 0.0)
    out = out + jnp.where(b == 0, up[at], rates[2, 0, below] * g[0, below])
    out = out + jnp.where(b == count - 1, down[at], rates[3, 0, above] * g[0, above])
    out = out + prev_c(rates[4, 0, b] * own, gz_before[2 * at, pl.ds(b, 1), :], row)
    out = out + next_c(rates[5, 0, b] * own, gz_after[2 * at + 1, pl.ds(b, 1), :], row)
    out = out + prev_d(rates[6, 0, b] * own, unpack_d(wa_before[0, b]), lane)
    out = out + next_d(rates[7, 0, b] * own, unpack_d(wa_after[0, b]), lane)
    return out


def back_body(pair, parts, rates, f_ref, cot, g, u_before, u_after, *refs):
    u_row, refs = refs[:parts], refs[parts:]
    back_rows(pair, rates, f_ref, cot, g, u_before, u_after, u_row, *refs)


def back_rows(pair, rates, f_ref, cot, g, u_before, u_after, u_row, up, down, gz_before, gz_after, wa_before, wa_after, first,
              back, h_ref, w_ref, up_ref, down_ref, gz_ref, *v_refs):
    count, c, d = g.shape[1:]
    row, lane = iotas(c, d)

    half = len(v_refs) // 2
    cut = v_refs[0].shape[1]

    def step(b, v, shift, came=None):
        out = spread(rates, f_ref, cot[0, b], g, up, down, gz_before, gz_after, wa_before, wa_after, 1, b, row, lane)
        if came:
            out = out + came(b)
        else:
            out = out + u_before[0, b] + u_after[0, b]
        h = f_ref[0, b] * out
        back[0, b] = out
        h_ref[0, b] = h
        if pair:
            v[0][0, b - shift] = (rates[0, 0, b] + rates[1, 0, b]) * h
        else:
            v[0][0, b - shift] = rates[0, 0, b] * h
            v[1][0, b - shift] = rates[1, 0, b] * h
        w_ref[0, b] = pack_d(first[0, b], rates[7, 0, b] * h, rates[6, 0, b] * h, lane)
        gz_ref[0, pl.ds(b, 1), :] = first[0, b, c - 1 :, :]
        gz_ref[1, pl.ds(b, 1), :] = first[0, b, :1, :]
        gz_ref[2, pl.ds(b, 1), :] = (rates[4, 0, b] * h)[c - 1 :]
        gz_ref[3, pl.ds(b, 1), :] = (rates[5, 0, b] * h)[:1]

    if not pair:
        rows(0, cut, lambda b: step(b, v_refs[:half], 0))
        rows(cut, count, lambda b: step(b, v_refs[half:], cut))
    else:
        over = u_row[0].shape[1] - c

        def part(first, lines):
            return sum(ref[0, first : first + lines] for ref in u_row)

        def most(b):
            return u_before[0, pl.ds(pl.multiple_of(b * c, 8), c), :]

        def mixed(b):
            return jnp.concatenate([u_before[0, pl.ds(b * c, c - over), :], part(0, over)], axis=0)

        rows(0, cut, lambda b: step(b, v_refs[:half], 0, most))
        rows(cut, count - 2, lambda b: step(b, v_refs[half:], cut, most))
        step(count - 2, v_refs[half:], cut, mixed if over else most)
        step(count - 1, v_refs[half:], cut, lambda b: part(over, c))
    up_ref[0] = first[0, count - 1]
    up_ref[1] = rates[2, 0, count - 1] * h_ref[0, count - 1]
    down_ref[0] = first[0, 0]
    down_ref[1] = rates[3, 0, 0] * h_ref[0, 0]


def last_body(rates, f_ref, labels, g, h, s_ref, start, start_before, start_after, up0, down0, gz_before0, gz_after0, wa_before0,
              wa_after0, first, first_before, first_after, up1, down1, gz_before1, gz_after1, wa_before1, wa_after1, back, committor, out, partial):
    count, c, d = first.shape[1:]
    row, lane = iotas(c, d)

    def step(b):
        f = f_ref[0, b]
        near1 = [first_after[0, b], first_before[0, b]]
        near1 += neighbours(first, up1, down1, gz_before1, gz_after1, wa_before1, wa_after1, b, row, lane)
        s1 = f * sum(rates[k, 0, b] * near1[k] for k in range(8))
        label = labels[0, b]
        committor[0, b] = jnp.where(label == 0, KEEP * first[0, b] + s1, jnp.where(label == 2, 1.0, 0.0))
        near0 = [start_after[0, b], start_before[0, b]]
        near0 += neighbours(start, up0, down0, gz_before0, gz_after0, wa_before0, wa_after0, b, row, lane)
        avg1, avg0 = s1 * (1.0 / DAMP), s_ref[0, b] * (1.0 / DAMP)
        gb, hb = g[0, b], h[0, b]
        for k in range(8):
            out[k, 0, b] = gb * (near1[k] - avg1) + hb * (near0[k] - avg0)
        partial[0, b] = spread(rates, f_ref, back[0, b], h, up1, down1, gz_before1, gz_after1, wa_before1, wa_after1, 1, b, row, lane)

    rows(0, count, step)


def finish(grad, came):
    parts = [came[0]] if came[0] is came[1] else list(came)
    shape = came[0].shape

    def kernel(*refs):
        grad_ref, came_refs, (out, total, sem) = refs[0], refs[1:-3], refs[-3:]
        acc = grad_ref[0, : shape[1]]
        for ref in came_refs:
            acc = acc + ref[0]
        total[...] = acc
        copy = pltpu.make_async_copy(total, out.at[0, pl.ds(0, shape[1])], sem)
        copy.start()
        copy.wait()

    return pl.pallas_call(
        kernel,
        out_shape=jax.ShapeDtypeStruct(grad.shape, jnp.float32),
        in_specs=[pl.BlockSpec(memory_space=pltpu.VMEM)] * (1 + len(parts)),
        out_specs=pl.BlockSpec(memory_space=pl.ANY),
        scratch_shapes=[pltpu.VMEM(shape[1:], jnp.float32), pltpu.SemaphoreType.DMA],
        compiler_params=pltpu.CompilerParams(vmem_limit_bytes=4 * 1024 * 1024),
        name="finish",
    )(grad, *parts)


def on_device(start, rates, labels, cotangent):
    _, b, c, d = start.shape
    block = (1, b, c, d)
    cells = b * c * d
    pair = lax.axis_size("grp") == 2
    blocks = [block] * (1 if pair else 2)
    tail = max(2, b // 4)
    faces = [(2, c, d), (2, c, d), (4, b, d)]

    start_before, start_after = both_ways(start, start, "grp")
    f, g, w0, up, down, gz, *u = call(
        functools.partial(prepare_body, pair), "prepare", [rates, labels, cotangent, start], [block] * 3 + faces + ([(1, b * c - part_lines(c), d), (1, part_lines(c), d)] if pair else blocks), 20 * cells
    )
    u_before, u_after = both_ways(u[0], u[0] if pair else u[1], "grp")
    u_row = part_swap(u[1]) if pair else []
    up0, down0 = both_ways(up, down, "gy")
    gz_before0, gz_after0 = both_ways(gz, gz, "gz")
    wa0 = both_ways(w0, w0, "wa")

    first, s0 = call(
        functools.partial(forward_body, pair),
        "forward",
        [rates, f, labels, start, start_before, start_after, up0, down0, gz_before0, gz_after0, *wa0],
        [block] * 2,
        30 * cells,
    )
    first_before, first_after = both_ways(first, first, "grp")

    back, h, w1, up, down, gz, *v = call(
        functools.partial(back_body, pair, len(u_row)),
        "backward",
        [rates, f, cotangent, g, u_before, u_after, *u_row, up0, down0, gz_before0, gz_after0, *wa0, first],
        [block] * 3 + faces + [(1, b - tail, c, d)] * len(blocks) + [(1, tail, c, d)] * len(blocks),
        30 * cells,
    )
    most = both_ways(v[0], v[len(blocks) - 1], "grp")
    rest = both_ways(v[len(blocks)], v[-1], "grp")
    up1, down1 = both_ways(up, down, "gy")
    gz_before1, gz_after1 = both_ways(gz, gz, "gz")
    wa1 = both_ways(w1, w1, "wa")

    committor, grad_rates, grad = call(
        last_body,
        "last",
        [rates, f, labels, g, h, s0, start, start_before, start_after, up0, down0, gz_before0, gz_after0, *wa0,
         first, first_before, first_after, up1, down1, gz_before1, gz_after1, *wa1, back],
        [block, (8, 1, b, c, d), block],
        120 * cells,
    )
    last_rows = grad[:, b - tail :] + rest[0]
    if not pair:
        last_rows = last_rows + rest[1]
    grad_start = lax.dynamic_update_slice(finish(grad, most), last_rows, (0, b - tail, 0, 0))
    return committor, grad_start, grad_rates


def solution(mesh):
    placed = (
        P("grp", "gy", "gz", "wa"),
        P(None, "grp", "gy", "gz", "wa"),
        P("grp", "gy", "gz", "wa"),
        P("grp", "gy", "gz", "wa"),
    )
    return jax.shard_map(
        on_device,
        mesh=mesh,
        in_specs=placed,
        out_specs=(
            P("grp", "gy", "gz", "wa"),
            P("grp", "gy", "gz", "wa"),
            P(None, "grp", "gy", "gz", "wa"),
        ),
        check_vma=False,
    )
```
